32 devices in a mesh: groups: 1, row: 32 (over z, y, x, core), col: 1.
Axes of the slice: x: 2, y: 2, z: 4, core: 2. Of those that a mesh axis runs over, the one named last changes fastest.
Arguments:
- pair: bfloat16 [128, 128, 128], P(('groups', 'row'), 'col'), may hold values from -6 to 6
- token_mask: int32 [128], P('groups'), may hold values 0 or 1
- tri_in_weight: bfloat16 [128, 512], replicated, may hold values from -0.5 to 0.5
- tri_gate_weight: bfloat16 [128, 128], replicated, may hold values from -0.5 to 0.5
- tri_out_weight: bfloat16 [128, 128], replicated, may hold values from -0.5 to 0.5
- atom_act: bfloat16 [2048, 128], P(('groups', 'row')), may hold values from -6 to 6
- atom_cond: bfloat16 [2048, 128], P(('groups', 'row')), may hold values from -60 to 60
- atom_token: int32 [2048], P(('groups', 'row')), may hold values from 0 to 127, as said below
- atom_mask: int32 [2048], P(('groups', 'row')), may hold values from 0 to 1, as said below
- ada_weight: bfloat16 [128, 256], replicated, may hold values from -0.5 to 0.5
- qkv_weight: bfloat16 [128, 384], replicated, may hold values from -0.5 to 0.5
- bias_weight: bfloat16 [128, 4], replicated, may hold values from -0.5 to 0.5
- attn_out_weight: bfloat16 [128, 128], replicated, may hold values from -0.5 to 0.5
- ffn_in_weight: bfloat16 [128, 512], replicated, may hold values from -0.5 to 0.5
- ffn_out_weight: bfloat16 [256, 128], replicated, may hold values from -0.375 to 0.375
- agg_weight: bfloat16 [128, 384], replicated, may hold values from -0.5 to 0.5
Outputs:
- pair_out: bfloat16 [128, 128, 128], P(('groups', 'row'), 'col')
- atom_out: bfloat16 [2048, 128], P(('groups', 'row'))
- token_out: bfloat16 [128, 384], P(('groups', 'row'))
The draws below stay inside these ranges and needn't reach their ends.
Inputs may be any that keep to these rules, and one draw needn't show every extreme that they name: `atom_token`: Nondecreasing; slots r * 64 to (r + 1) * 64 - 1 hold the atoms of tokens r * 4 to (r + 1) * 4 - 1 followed by padding slots that name the last of those tokens; every token has 1 to 24 atoms. `atom_mask`: in each slab of 64 slots the atoms come first and at most 31 padding slots follow.
All inputs are finite; a program needn't handle non-finite values.
Results may differ from the reference program's by a relative error of at most 0.012.
The reference program's roundings to bfloat16 on the way count: a program that leaves them out, or rounds other values in their place, can miss the bound.
Values may be sent and summed in bfloat16 or wider, within the bound.
A program may use at most 64 MiB of HBM per device.

```python
import math
import jax
import jax.numpy as jnp
from jax import lax

PAIR_CH = 128
ATOM_CH = 128
SINGLE_CH = 384
HEADS = 4
FFA = 256
QUERY_WINDOW = 32
KEYS = 128
MAXAT = 24
TOK_ROW = 4
N_TOK = 128
ATOM_ROW = 64
ATOMS = 2048
N_ROW = 32


def slab_layout(key):
    devices = ATOMS // ATOM_ROW
    first, second, third, fourth = jax.random.split(jax.random.fold_in(key, 11), 4)
    lowest = ATOM_ROW - QUERY_WINDOW + 1
    totals = jax.random.randint(first, (devices,), lowest, ATOM_ROW + 1)
    fullest = jax.random.randint(second, (), 0, devices)
    totals = jnp.where(jnp.arange(devices) == fullest, ATOM_ROW, totals)
    spare = MAXAT - 1
    slots = TOK_ROW * spare
    owners = jnp.arange(slots) // spare
    favored = jax.random.randint(third, (devices, 1), 0, TOK_ROW)
    noise = jax.random.randint(fourth, (devices, slots), 1, 1 << 20)
    logit_scores = jnp.where(owners[None, :] == favored, 0, noise) * slots + jnp.arange(slots)[None, :]
    ranks = jnp.argsort(jnp.argsort(logit_scores, axis=1), axis=1)
    extra = (totals - TOK_ROW)[:, None]
    chosen = (ranks < extra).astype(jnp.int32)
    counts = 1 + jnp.sum(chosen.reshape(devices, TOK_ROW, spare), axis=2)
    bounds = jnp.cumsum(counts, axis=1)
    position = jnp.arange(ATOM_ROW)
    local = jnp.sum((position[None, :, None] >= bounds[:, None, :]).astype(jnp.int32), axis=2)
    local = jnp.minimum(local, TOK_ROW - 1)
    owner_tokens = jnp.arange(devices)[:, None] * TOK_ROW + local
    live = (position[None, :] < totals[:, None]).astype(jnp.int32)
    return (owner_tokens.reshape(-1).astype(jnp.int32), live.reshape(-1).astype(jnp.int32))


def draw_atom_token(key, part):
    return slab_layout(key)[0]


def draw_atom_mask(key, part):
    return slab_layout(key)[1]


def draw_atom_cond(key, part):
    first = jax.random.fold_in(jax.random.fold_in(key, 23), 0)
    shape = (ATOMS, ATOM_CH)
    values = jax.random.normal(first, shape, jnp.float32)
    return jnp.clip(values, -60.0, 60.0).astype(jnp.bfloat16)


def touch_ends(values, rng, smallest, largest):
    place = [jax.random.randint(jax.random.fold_in(rng, axis), (), 0, length) for axis, length in enumerate(values.shape)]
    main_axis = values.shape.index(max(values.shape))
    neighbour = place[:main_axis] + [(place[main_axis] + 1) % values.shape[main_axis]] + place[main_axis + 1:]
    return values.at[tuple(place)].set(smallest).at[tuple(neighbour)].set(largest)


def shard_levels(key, dims, cuts, low, top_value):
    loudness = 1.0
    for dim, parts in cuts:
        draws = jax.random.uniform(jax.random.fold_in(jax.random.fold_in(key, 6), dim), (parts,), jnp.float32, low / len(cuts), top_value / len(cuts))
        loudness = loudness * jnp.repeat(jnp.exp(draws), dims[dim] // parts).reshape((-1,) + (1,) * (len(dims) - 1 - dim))
    return loudness


def bell_draw(rng, extent, scale, most, pieces=(), kind=jnp.bfloat16):
    drawn = scale * jax.random.normal(rng, extent, jnp.float32)
    if pieces:
        drawn = drawn * shard_levels(rng, extent, pieces, -0.22, 0.18)
    return jnp.clip(drawn, -most, most).astype(kind)


def setup_inputs(seed: int = 0, part: int = 0) -> dict:
    key_of = jax.random.split(jax.random.key(seed), 17)
    own_keys = jax.random.split(jax.random.fold_in(key_of[16], part), 17)
    return {
        "pair": bell_draw(own_keys[0], (N_TOK, N_TOK, PAIR_CH), 1.0, 6.0, ((0, 32),)),
        "token_mask": touch_ends((jax.random.randint(own_keys[1], (N_TOK,), 0, 8) < 7).astype(jnp.int32), jax.random.fold_in(own_keys[1], 1), 0, 1),
        "tri_in_weight": bell_draw(key_of[2], (PAIR_CH, 4 * PAIR_CH), PAIR_CH ** -0.5, 0.5),
        "tri_gate_weight": bell_draw(key_of[3], (PAIR_CH, PAIR_CH), PAIR_CH ** -0.5, 0.5),
        "tri_out_weight": bell_draw(key_of[4], (PAIR_CH, PAIR_CH), PAIR_CH ** -0.5, 0.5),
        "atom_act": bell_draw(own_keys[5], (ATOMS, ATOM_CH), 1.0, 6.0, ((0, 32),)),
        "atom_cond": draw_atom_cond(jax.random.fold_in(jax.random.fold_in(key_of[16], part), 71), part),
        "atom_token": draw_atom_token(jax.random.fold_in(jax.random.fold_in(key_of[16], part), 71), part),
        "atom_mask": draw_atom_mask(jax.random.fold_in(jax.random.fold_in(key_of[16], part), 71), part),
        "ada_weight": bell_draw(key_of[9], (ATOM_CH, 2 * ATOM_CH), ATOM_CH ** -0.5, 0.5),
        "qkv_weight": bell_draw(key_of[10], (ATOM_CH, 3 * ATOM_CH), ATOM_CH ** -0.5, 0.5),
        "bias_weight": bell_draw(key_of[11], (PAIR_CH, HEADS), PAIR_CH ** -0.5, 0.5),
        "attn_out_weight": bell_draw(key_of[12], (ATOM_CH, ATOM_CH), ATOM_CH ** -0.5, 0.5),
        "ffn_in_weight": bell_draw(key_of[13], (ATOM_CH, 2 * FFA), ATOM_CH ** -0.5, 0.5),
        "ffn_out_weight": bell_draw(key_of[14], (FFA, ATOM_CH), FFA ** -0.5, 0.375),
        "agg_weight": bell_draw(key_of[15], (ATOM_CH, SINGLE_CH), ATOM_CH ** -0.5, 0.5),
    }


EPSILON = 1e-05

def layer_norm(values, along):
    average = lax.optimization_barrier(jnp.mean(values, axis=along, keepdims=True))
    centred = values - average
    spread = lax.optimization_barrier(jnp.mean(centred * centred, axis=along, keepdims=True))
    return centred / jnp.sqrt(spread + EPSILON)

def reference(pair, token_mask, tri_in_weight, tri_gate_weight, tri_out_weight, atom_act, atom_cond, atom_token, atom_mask, ada_weight, qkv_weight, bias_weight, attn_out_weight, ffn_in_weight, ffn_out_weight, agg_weight):
    tokens = pair.shape[0]
    channels = pair.shape[2]
    rows = tokens // N_ROW
    token_live = token_mask.astype(jnp.float32)
    in_weight = tri_in_weight.astype(jnp.float32)

    def project_block(index):
        start = index * rows
        block = lax.dynamic_slice_in_dim(pair, start, rows, 0).astype(jnp.float32)
        normed = layer_norm(block, 2).astype(jnp.bfloat16).astype(jnp.float32)
        terms = jnp.einsum('ijd,de->ije', normed, in_weight)
        row_live = lax.dynamic_slice_in_dim(token_live, start, rows, 0)
        both = row_live[:, None, None] * token_live[None, :, None]
        left = (jax.nn.sigmoid(terms[..., channels:2 * channels]) * terms[..., :channels] * both).astype(jnp.bfloat16)
        right = (jax.nn.sigmoid(terms[..., 3 * channels:]) * terms[..., 2 * channels:3 * channels] * both).astype(jnp.bfloat16)
        return (left, right)
    left, right = lax.map(project_block, jnp.arange(N_ROW, dtype=jnp.int32))
    left = left.reshape(tokens, tokens, channels).transpose(2, 0, 1)
    right = right.reshape(tokens, tokens, channels).transpose(2, 0, 1)

    def contract(index):
        return jnp.dot(left[index], right[index].T, preferred_element_type=jnp.float32).astype(jnp.bfloat16)
    product = lax.map(contract, jnp.arange(channels, dtype=jnp.int32))

    def finish_block(index):
        start = index * rows
        block = lax.dynamic_slice_in_dim(pair, start, rows, 0).astype(jnp.float32)
        normed = layer_norm(block, 2).astype(jnp.bfloat16).astype(jnp.float32)
        gate = jax.nn.sigmoid(jnp.einsum('ijd,de->ije', normed, tri_gate_weight.astype(jnp.float32)))
        summed = lax.dynamic_slice_in_dim(product, start, rows, 1).astype(jnp.float32)
        summed_norm = layer_norm(summed, 0).astype(jnp.bfloat16).astype(jnp.float32)
        update = jnp.einsum('dij,de->ije', summed_norm, tri_out_weight.astype(jnp.float32))
        return (block + gate * update).astype(jnp.bfloat16)
    pair_out = lax.map(finish_block, jnp.arange(N_ROW, dtype=jnp.int32)).reshape(tokens, tokens, channels)
    atoms = atom_act.shape[0]
    window_width = atom_act.shape[1]
    head_size = window_width // HEADS
    side = (KEYS - QUERY_WINDOW) // 2
    live = atom_mask.astype(jnp.float32)
    ada = jnp.dot(atom_cond, ada_weight, preferred_element_type=jnp.float32)
    atom_inputs = (jax.nn.sigmoid(ada[:, :window_width]) * layer_norm(atom_act.astype(jnp.float32), 1) + ada[:, window_width:]).astype(jnp.bfloat16)
    projected = jnp.dot(atom_inputs, qkv_weight, preferred_element_type=jnp.float32).astype(jnp.bfloat16)
    queries = projected[:, :window_width]
    padded_keys = jnp.pad(projected[:, window_width:], ((side, side), (0, 0)))
    key_live = jnp.pad(live, (side, side))
    key_token = jnp.pad(atom_token, (side, side))

    def attend(window):
        start = window * QUERY_WINDOW
        query_rows = lax.dynamic_slice_in_dim(queries, start, QUERY_WINDOW, 0).astype(jnp.float32).reshape(QUERY_WINDOW, HEADS, head_size)
        key_rows = lax.dynamic_slice_in_dim(padded_keys, start, KEYS, 0).astype(jnp.float32)
        window_key_rows = key_rows[:, :window_width].reshape(KEYS, HEADS, head_size)
        window_value_rows = key_rows[:, window_width:].reshape(KEYS, HEADS, head_size)
        query_token = lax.dynamic_slice_in_dim(atom_token, start, QUERY_WINDOW, 0)
        keys_token = lax.dynamic_slice_in_dim(key_token, start, KEYS, 0)
        keys_live = lax.dynamic_slice_in_dim(key_live, start, KEYS, 0)
        block = pair_out[query_token][:, keys_token].astype(jnp.float32)
        bias_norm = layer_norm(block, 2).astype(jnp.bfloat16)
        pair_tile_bias = jnp.dot(bias_norm.reshape(QUERY_WINDOW * KEYS, channels), bias_weight, preferred_element_type=jnp.float32).astype(jnp.bfloat16)
        pair_tile_bias = pair_tile_bias.astype(jnp.float32).reshape(QUERY_WINDOW, KEYS, HEADS).transpose(2, 0, 1)
        logit_scores = jnp.einsum('zki,uki->kzu', query_rows, window_key_rows) / math.sqrt(head_size) + pair_tile_bias
        logit_scores = jnp.where(keys_live[None, None, :] > 0, logit_scores, -1e+30)
        softmax_weight = jax.nn.softmax(logit_scores, axis=-1).astype(jnp.bfloat16).astype(jnp.float32)
        head_mixture = jnp.einsum('fkn,nfv->kfv', softmax_weight, window_value_rows).reshape(QUERY_WINDOW, window_width)
        return head_mixture.astype(jnp.bfloat16)
    attended = lax.map(attend, jnp.arange(atoms // QUERY_WINDOW, dtype=jnp.int32)).reshape(atoms, window_width)
    atom_mid = atom_act.astype(jnp.float32) + jnp.dot(attended, attn_out_weight, preferred_element_type=jnp.float32)
    atom_norm = layer_norm(atom_mid, 1).astype(jnp.bfloat16)
    expanded = jnp.dot(atom_norm, ffn_in_weight, preferred_element_type=jnp.float32)
    hidden_width = ffn_out_weight.shape[0]
    inner = (jax.nn.silu(expanded[:, :hidden_width]) * expanded[:, hidden_width:]).astype(jnp.bfloat16)
    atom_out = ((atom_mid + jnp.dot(inner, ffn_out_weight, preferred_element_type=jnp.float32)) * live[:, None]).astype(jnp.bfloat16)
    features = jax.nn.relu(jnp.dot(atom_out, agg_weight, preferred_element_type=jnp.float32)).astype(jnp.bfloat16)
    sums = jax.ops.segment_sum(features.astype(jnp.float32) * live[:, None], atom_token, num_segments=tokens)
    counts = jax.ops.segment_sum(live, atom_token, num_segments=tokens)
    token_out = (sums / counts[:, None]).astype(jnp.bfloat16)
    return (pair_out, atom_out, token_out)
```

```python
import functools
import math

import jax
import jax.numpy as jnp
from jax import lax
from jax.experimental import pallas as pl
from jax.experimental.pallas import tpu as pltpu
from jax.sharding import PartitionSpec as P

QUERY_WINDOW = 32
KEYS = 128


EPSILON = 1e-05


def extended(shard, sides, width):
    for axis, dim in sides:
        size, length = (lax.axis_size(axis), shard.shape[dim])
        up = [(i, (i + 1) % size) for i in range(size - 1)]
        down = [(j, i) for i, j in up]
        last = lax.slice_in_dim(shard, length - width, length, axis=dim)
        first = lax.slice_in_dim(shard, 0, width, axis=dim)
        before = lax.ppermute(last, axis, up)
        after = lax.ppermute(first, axis, down)
        shard = jnp.concatenate([before, shard, after], axis=dim)
    return shard


def layer_norm(values, along):
    average = jnp.mean(values, axis=along, keepdims=True)
    centred = values - average
    spread = jnp.mean(centred * centred, axis=along, keepdims=True)
    return centred / jnp.sqrt(spread + EPSILON)


def spread_device(
    pair,
    token_mask,
    tri_in_weight,
    tri_gate_weight,
    tri_out_weight,
    atom_act,
    atom_cond,
    atom_token,
    atom_mask,
    ada_weight,
    qkv_weight,
    bias_weight,
    attn_out_weight,
    ffn_in_weight,
    ffn_out_weight,
    agg_weight,
):
    tok_rows = pair.shape[0]
    col_count = pair.shape[1]
    channels = pair.shape[2]
    row_index = lax.axis_index("row")
    col_index = lax.axis_index("col")
    pair_float = pair.astype(jnp.float32)
    pair_norm = layer_norm(pair_float, 2).astype(jnp.bfloat16)
    row_live = lax.dynamic_slice_in_dim(token_mask, row_index * tok_rows, tok_rows, 0).astype(
        jnp.float32
    )
    col_live = lax.dynamic_slice_in_dim(token_mask, col_index * col_count, col_count, 0).astype(
        jnp.float32
    )
    pair_live = row_live[:, None] * col_live[None, :]
    left_terms = jnp.einsum(
        "ijd,de->eij",
        pair_norm,
        tri_in_weight[:, : 2 * channels],
        preferred_element_type=jnp.float32,
    )
    left = (jax.nn.sigmoid(left_terms[channels:]) * left_terms[:channels] * pair_live).astype(
        jnp.bfloat16
    )
    right_terms = jnp.einsum(
        "ijd,de->eij",
        pair_norm,
        tri_in_weight[:, 2 * channels :],
        preferred_element_type=jnp.float32,
    )
    right = (jax.nn.sigmoid(right_terms[channels:]) * right_terms[:channels] * pair_live).astype(
        jnp.bfloat16
    )
    tri_gate = jax.nn.sigmoid(
        jnp.einsum("ijd,de->ije", pair_norm, tri_gate_weight, preferred_element_type=jnp.float32)
    )
    left_owned, right_owned = (
        lax.all_to_all(left, "row", split_axis=0, concat_axis=1, tiled=True),
        lax.all_to_all(right, "row", split_axis=0, concat_axis=1, tiled=True),
    )
    left_full, right_rows = (
        lax.all_gather(left_owned, "col", axis=2, tiled=True),
        lax.all_gather(right_owned, "col", axis=2, tiled=True),
    )
    right_used = lax.dynamic_slice_in_dim(right_rows, col_index * col_count, col_count, 1)
    tri_sum = jnp.einsum(
        "cik,cjk->cij", left_full, right_used, preferred_element_type=jnp.float32
    ).astype(jnp.bfloat16)
    merged = lax.all_to_all(tri_sum, "row", split_axis=1, concat_axis=0, tiled=True)
    tri_norm = layer_norm(merged.astype(jnp.float32), 0).astype(jnp.bfloat16)
    update = jnp.einsum("dij,de->ije", tri_norm, tri_out_weight, preferred_element_type=jnp.float32)
    pair_out = (pair_float + tri_gate * update).astype(jnp.bfloat16)
    band_width = 3 * tok_rows
    targets = (row_index - 1) * tok_rows + jnp.arange(band_width, dtype=jnp.int32)
    columns = col_index * col_count + jnp.arange(col_count, dtype=jnp.int32)
    selector = (columns[:, None] == targets[None, :]).astype(jnp.bfloat16)
    band_part = jnp.einsum("ijd,jb->ibd", pair_out, selector, preferred_element_type=jnp.float32)
    band = lax.psum(band_part.astype(jnp.bfloat16), "col").astype(jnp.float32)
    band_norm = layer_norm(band, 2).astype(jnp.bfloat16)
    bias_table = jnp.einsum(
        "ibd,dh->ibh", band_norm, bias_weight, preferred_element_type=jnp.float32
    ).astype(jnp.bfloat16)
    slab = atom_act.shape[0]
    window_width = atom_act.shape[1]
    heads = bias_weight.shape[1]
    head_size = window_width // heads
    side = (KEYS - QUERY_WINDOW) // 2
    windows = slab // QUERY_WINDOW
    local_token = atom_token - row_index * tok_rows
    live = atom_mask.astype(jnp.float32)
    token_tag = ((local_token + 1) * atom_mask).astype(jnp.bfloat16)
    ada = jnp.dot(atom_cond, ada_weight, preferred_element_type=jnp.float32)
    atom_inputs = (
        jax.nn.sigmoid(ada[:, :window_width]) * layer_norm(atom_act.astype(jnp.float32), 1)
        + ada[:, window_width:]
    ).astype(jnp.bfloat16)
    projected = jnp.dot(atom_inputs, qkv_weight, preferred_element_type=jnp.float32).astype(
        jnp.bfloat16
    )
    queries = projected[:, :window_width]
    ext_pairs, ext_tag = (
        extended(projected[:, window_width:], (("row", 0),), side),
        extended(token_tag, (("row", 0),), side),
    )
    ext_rows = slab + 2 * side
    ext_position = jnp.arange(ext_rows, dtype=jnp.int32)
    offset = jnp.where(
        ext_position < side, 0, jnp.where(ext_position < side + slab, tok_rows, 2 * tok_rows)
    )
    tag_value = ext_tag.astype(jnp.int32)
    key_valid = tag_value > 0
    band_index = tag_value - 1 + offset
    band_slots = jnp.arange(band_width, dtype=jnp.int32)
    key_onehot = ((band_index[:, None] == band_slots[None, :]) & key_valid[:, None]).astype(
        jnp.bfloat16
    )
    query_onehot = (local_token[:, None] == jnp.arange(tok_rows, dtype=jnp.int32)[None, :]).astype(
        jnp.bfloat16
    )
    query_bias = jnp.einsum(
        "lt,tbh->lbh", query_onehot, bias_table, preferred_element_type=jnp.float32
    ).astype(jnp.bfloat16)
    query_bias = query_bias.reshape(windows, QUERY_WINDOW, band_width, heads)
    key_index = (
        jnp.arange(windows, dtype=jnp.int32)[:, None] * QUERY_WINDOW
        + jnp.arange(KEYS, dtype=jnp.int32)[None, :]
    )
    window_pairs = ext_pairs[key_index]
    window_onehot = key_onehot[key_index]
    window_valid = key_valid[key_index]
    window_bias = jnp.einsum(
        "wlbh,wmb->whlm", query_bias, window_onehot, preferred_element_type=jnp.float32
    )
    query_heads = queries.reshape(windows, QUERY_WINDOW, heads, head_size)
    key_heads = window_pairs[..., :window_width].reshape(windows, KEYS, heads, head_size)
    value_heads = window_pairs[..., window_width:].reshape(windows, KEYS, heads, head_size)
    logit_scores = (
        jnp.einsum("wlhd,wmhd->whlm", query_heads, key_heads, preferred_element_type=jnp.float32)
        / math.sqrt(head_size)
        + window_bias
    )
    logit_scores = jnp.where(window_valid[:, None, None, :], logit_scores, -1e30)
    attn_weights = jax.nn.softmax(logit_scores, axis=-1).astype(jnp.bfloat16)
    attended = (
        jnp.einsum("whlm,wmhd->wlhd", attn_weights, value_heads, preferred_element_type=jnp.float32)
        .reshape(slab, window_width)
        .astype(jnp.bfloat16)
    )
    atom_mid = atom_act.astype(jnp.float32) + jnp.dot(
        attended, attn_out_weight, preferred_element_type=jnp.float32
    )
    atom_norm = layer_norm(atom_mid, 1).astype(jnp.bfloat16)
    expanded = jnp.dot(atom_norm, ffn_in_weight, preferred_element_type=jnp.float32)
    hidden_width = ffn_out_weight.shape[0]
    inner = (jax.nn.silu(expanded[:, :hidden_width]) * expanded[:, hidden_width:]).astype(
        jnp.bfloat16
    )
    atom_out = (
        (atom_mid + jnp.dot(inner, ffn_out_weight, preferred_element_type=jnp.float32))
        * live[:, None]
    ).astype(jnp.bfloat16)
    features = jax.nn.relu(
        jnp.dot(atom_out, agg_weight, preferred_element_type=jnp.float32)
    ).astype(jnp.bfloat16)
    live_onehot = query_onehot * atom_mask.astype(jnp.bfloat16)[:, None]
    token_sums = jnp.einsum("at,ac->tc", live_onehot, features, preferred_element_type=jnp.float32)
    token_counts = jnp.sum(live_onehot.astype(jnp.float32), axis=0)
    token_out = (token_sums / token_counts[:, None]).astype(jnp.bfloat16)
    return (pair_out, atom_out, token_out)


MESH = pl.DeviceIdType.MESH
F32 = jnp.float32
BF16 = jnp.bfloat16


def dot_nn(a, b):
    return lax.dot_general(a, b, (((1,), (0,)), ((), ())), preferred_element_type=F32)


def dot_nt(a, b):
    return lax.dot_general(a, b, (((1,), (1,)), ((), ())), preferred_element_type=F32)


def dot_tn(a, b):
    return lax.dot_general(a, b, (((0,), (0,)), ((), ())), preferred_element_type=F32)


def normed(values, along):
    average = jnp.mean(values, axis=along, keepdims=True)
    centred = values - average
    spread = jnp.mean(centred * centred, axis=along, keepdims=True)
    return centred * lax.rsqrt(spread + EPSILON)


def fused_kernel(
    sizes,
    pair,
    token_mask,
    tri_in_weight,
    tri_gate_weight,
    tri_out_weight,
    atom_act,
    atom_cond,
    atom_token,
    atom_mask,
    ada_weight,
    qkv_weight,
    bias_weight,
    attn_out_weight,
    ffn_in_weight,
    ffn_out_weight,
    agg_weight,
    pair_out,
    atom_out,
    token_out,
    terms_wide,
    send_terms,
    recv_terms,
    left_wide,
    right_wide,
    sums_wide,
    send_sums,
    recv_sums,
    gate_ref,
    rim,
    send_sem,
    recv_sem,
    rim_send,
    rim_recv,
):
    devices, tok_rows, tokens, channels, owned, slab, heads = sizes
    block = tok_rows * owned
    side = (KEYS - QUERY_WINDOW) // 2
    ext = slab + 2 * side
    group = lax.axis_index("groups")
    me = lax.axis_index("row")
    col = lax.axis_index("col")

    barrier = pltpu.get_barrier_semaphore()

    def greet(step, carry):
        peer = lax.rem(me + step, devices)
        pl.semaphore_signal(barrier, inc=1, device_id=(group, peer, col), device_id_type=MESH)
        return carry

    lax.fori_loop(1, devices, greet, 0)

    mask_row = token_mask[...].astype(F32)
    lane = lax.broadcasted_iota(jnp.int32, (1, tokens), 1)
    in_weight = tri_in_weight[...].T
    for i in range(tok_rows):
        norm = normed(pair[i].astype(F32), 1).astype(BF16)
        row_mask = jnp.sum(jnp.where(lane == me * tok_rows + i, mask_row, 0.0), axis=1, keepdims=True)
        both = row_mask * mask_row
        terms = dot_nt(in_weight, norm)
        for part in range(2):
            base = part * 2 * channels
            value = (
                jax.nn.sigmoid(terms[base + channels : base + 2 * channels])
                * terms[base : base + channels]
                * both
            )
            for c in range(owned):
                terms_wide[part, pl.ds(i * owned + c, devices, stride=block), :] = value[
                    c * devices : (c + 1) * devices
                ]
        gate_ref[i] = jax.nn.sigmoid(dot_nn(norm, tri_gate_weight[...]))
    for part in range(2):
        send_terms[:, part] = terms_wide[part].reshape(devices, block, tokens).astype(BF16)

    pl.semaphore_wait(barrier, devices - 1)

    def terms_copy(peer):
        return pltpu.make_async_remote_copy(
            src_ref=send_terms.at[peer],
            dst_ref=recv_terms.at[me],
            send_sem=send_sem.at[0],
            recv_sem=recv_sem.at[0],
            device_id=(group, peer, col),
            device_id_type=MESH,
        )

    def send_first(step, carry):
        terms_copy(lax.rem(me + step, devices)).start()
        return carry

    lax.fori_loop(1, devices, send_first, 0)
    recv_terms[me] = send_terms[me]

    token_row = atom_token[...] - me * tok_rows
    live_row = atom_mask[...]
    wide = (channels, slab)
    token_col = jnp.broadcast_to(token_row.astype(F32), wide).T
    live_col = jnp.broadcast_to(live_row.astype(F32), wide).T
    act = atom_act[...].astype(F32)
    ada = dot_nn(atom_cond[...], ada_weight[...])
    width = act.shape[1]
    atom_inputs = (jax.nn.sigmoid(ada[:, :width]) * normed(act, 1) + ada[:, width:]).astype(BF16)
    projected = dot_nn(atom_inputs, qkv_weight[...]).astype(BF16)
    rim[side : side + slab, : 2 * width] = projected[:, width:]
    rim[side : side + slab, 2 * width :] = ((token_col + 1.0) * live_col).astype(BF16)

    up = pltpu.make_async_remote_copy(
        src_ref=rim.at[pl.ds(slab, side)],
        dst_ref=rim.at[pl.ds(0, side)],
        send_sem=rim_send.at[0],
        recv_sem=rim_recv.at[0],
        device_id=(group, lax.rem(me + 1, devices), col),
        device_id_type=MESH,
    )
    down = pltpu.make_async_remote_copy(
        src_ref=rim.at[pl.ds(side, side)],
        dst_ref=rim.at[pl.ds(side + slab, side)],
        send_sem=rim_send.at[1],
        recv_sem=rim_recv.at[1],
        device_id=(group, lax.rem(me + devices - 1, devices), col),
        device_id_type=MESH,
    )

    @pl.when(me < devices - 1)
    def _():
        up.start()

    @pl.when(me > 0)
    def _():
        down.start()

    @pl.when(me == 0)
    def _():
        rim[:side] = jnp.zeros((side, rim.shape[1]), BF16)

    @pl.when(me == devices - 1)
    def _():
        rim[side + slab :] = jnp.zeros((side, rim.shape[1]), BF16)

    others = pl.ds(0, devices - 1)
    pltpu.make_async_copy(send_terms.at[others], recv_terms.at[others], recv_sem.at[0]).wait()
    left_wide[...] = recv_terms[:, 0].reshape(devices * block, tokens).astype(F32)
    right_wide[...] = recv_terms[:, 1].reshape(devices * block, tokens).astype(F32)
    for c in range(owned):
        rows = pl.ds(c, tokens, stride=owned)
        sums_wide[rows, :] = dot_nt(
            left_wide[rows, :].astype(BF16), right_wide[rows, :].astype(BF16)
        )
    send_sums[...] = sums_wide[...].reshape(devices, block, tokens).astype(BF16)

    def sums_copy(peer):
        return pltpu.make_async_remote_copy(
            src_ref=send_sums.at[peer],
            dst_ref=recv_sums.at[me],
            send_sem=send_sem.at[1],
            recv_sem=recv_sem.at[1],
            device_id=(group, peer, col),
            device_id_type=MESH,
        )

    def send_second(step, carry):
        sums_copy(lax.rem(me + step, devices)).start()
        return carry

    lax.fori_loop(1, devices, send_second, 0)
    recv_sums[me] = send_sums[me]

    @pl.when(me > 0)
    def _():
        up.wait_recv()

    @pl.when(me < devices - 1)
    def _():
        down.wait_recv()

    head_size = width // heads
    keys = rim[:, :width]
    values = rim[:, width : 2 * width]
    tag = rim[:, 2 * width :].astype(F32)
    head_lane = lax.broadcasted_iota(jnp.int32, (slab, width), 1) // head_size
    queries = projected[:, :width].astype(F32)
    split_queries = jnp.concatenate(
        [jnp.where(head_lane == h, queries, 0.0) for h in range(heads)], axis=0
    ).astype(BF16)
    raw_scores = dot_nt(split_queries, keys) * (1.0 / math.sqrt(head_size))
    band = 4 * tok_rows
    dead_lane = tok_rows * band
    ext_row = lax.broadcasted_iota(jnp.int32, (ext, channels), 0)
    ext_lane = lax.broadcasted_iota(jnp.int32, (ext, channels), 1)
    offset = jnp.where(
        ext_row < side, 0, jnp.where(ext_row < side + slab, tok_rows, 2 * tok_rows)
    )
    band_index = tag.astype(jnp.int32) - 1 + offset
    slot = lax.rem(ext_lane, band)
    alive = tag > 0.0
    key_map = jnp.where(
        ext_lane < dead_lane,
        jnp.where(alive & (band_index == slot), 1.0, 0.0),
        jnp.where(alive, 0.0, 1.0),
    ).astype(BF16)
    query_lane = lax.broadcasted_iota(jnp.int32, (slab, channels), 1)
    query_map = jnp.where(
        (query_lane // band == token_col.astype(jnp.int32)) | (query_lane == dead_lane), 1.0, 0.0
    )
    score_row = lax.broadcasted_iota(jnp.int32, (slab, ext), 0) // QUERY_WINDOW * QUERY_WINDOW
    score_lane = lax.broadcasted_iota(jnp.int32, (slab, ext), 1)
    in_window = (score_lane >= score_row) & (score_lane < score_row + KEYS)

    pltpu.make_async_copy(send_sums.at[others], recv_sums.at[others], recv_sem.at[1]).wait()
    sums_wide[...] = recv_sums[...].reshape(devices * block, tokens).astype(F32)
    band_row = lax.broadcasted_iota(jnp.int32, (band, tokens), 0)
    band_lane = lax.broadcasted_iota(jnp.int32, (band, tokens), 1)
    selector = jnp.where(
        (band_lane == (me - 1) * tok_rows + band_row) & (band_row < 3 * tok_rows), 1.0, 0.0
    ).astype(BF16)
    bands = []
    for i in range(tok_rows):
        merged = jnp.concatenate(
            [
                sums_wide[pl.ds(i * owned + c, devices, stride=block), :]
                for c in range(owned)
            ],
            axis=0,
        )
        tri_norm = normed(merged, 0).T.astype(BF16)
        update = dot_nn(tri_norm, tri_out_weight[...])
        updated = (pair[i].astype(F32) + gate_ref[i] * update).astype(BF16)
        pair_out[i] = updated
        bands.append(dot_nn(selector, updated))
    bands.append(jnp.zeros((channels - tok_rows * band, channels), F32))
    band_norm = normed(jnp.concatenate(bands, axis=0), 1).astype(BF16)
    table = dot_nt(bias_weight[...].astype(F32).T.astype(BF16), band_norm).astype(BF16).astype(F32)
    table_lane = lax.broadcasted_iota(jnp.int32, table.shape, 1)
    table = jnp.where(table_lane == dead_lane, -1e30, table)
    bias_rows = jnp.concatenate(
        [query_map * table[h : h + 1] for h in range(heads)], axis=0
    ).astype(BF16)
    scores = raw_scores + dot_nt(bias_rows, key_map)
    scores = jnp.where(jnp.concatenate([in_window] * heads, axis=0), scores, -1e30)
    scores = jnp.exp(scores - jnp.max(scores, axis=1, keepdims=True))
    weights = (scores / jnp.sum(scores, axis=1, keepdims=True)).astype(BF16)
    mixed = dot_nn(weights, values)
    attended = jnp.zeros((slab, width), F32)
    for h in range(heads):
        attended = jnp.where(head_lane == h, mixed[h * slab : (h + 1) * slab], attended)
    atom_mid = act + dot_nn(attended.astype(BF16), attn_out_weight[...])
    expanded = dot_nn(normed(atom_mid, 1).astype(BF16), ffn_in_weight[...])
    hidden = ffn_out_weight.shape[0]
    up_part, gate_part = expanded[:, hidden:], expanded[:, :hidden]
    inner = (gate_part * jax.nn.sigmoid(gate_part) * up_part).astype(BF16)
    result = ((atom_mid + dot_nn(inner, ffn_out_weight[...])) * live_col).astype(BF16)
    atom_out[...] = result
    features = jnp.maximum(dot_nn(result, agg_weight[...]), 0.0).astype(BF16)
    owner_row = lax.broadcasted_iota(jnp.int32, (tok_rows, slab), 0)
    owner = jnp.where((owner_row == token_row) & (live_row > 0), 1.0, 0.0)
    counts = jnp.sum(owner, axis=1, keepdims=True)
    token_out[...] = (dot_nn(owner.astype(BF16), features) / counts).astype(BF16)

    pltpu.make_async_copy(send_terms.at[others], recv_terms.at[others], send_sem.at[0]).wait()
    pltpu.make_async_copy(send_sums.at[others], recv_sums.at[others], send_sem.at[1]).wait()

    @pl.when(me < devices - 1)
    def _():
        up.wait_send()

    @pl.when(me > 0)
    def _():
        down.wait_send()


def per_device(*args):
    pair, token_mask, atom_act, atom_token = args[0], args[1], args[5], args[7]
    tok_rows, tokens, channels = pair.shape
    slab, width = atom_act.shape
    heads = args[11].shape[1]
    devices = lax.axis_size("row")
    owned = channels // devices
    block = tok_rows * owned
    fits = (
        lax.axis_size("col") == 1
        and owned * devices == channels
        and block % 16 == 0
        and slab % QUERY_WINDOW == 0
        and devices % 8 == 0
        and width == channels
        and 4 * tok_rows % 16 == 0
        and 4 * tok_rows * tok_rows < channels
        and slab >= (KEYS - QUERY_WINDOW) // 2
    )
    if not fits:
        return spread_device(*args)
    side = (KEYS - QUERY_WINDOW) // 2
    args = list(args)
    for k in (1, 7, 8):
        args[k] = args[k].reshape(1, -1)
    agg_width = args[15].shape[1]
    sizes = (devices, tok_rows, tokens, channels, owned, slab, heads)
    in_vmem = pl.BlockSpec(memory_space=pltpu.VMEM)
    return tuple(
        pl.pallas_call(
            functools.partial(fused_kernel, sizes),
            out_shape=(
                jax.ShapeDtypeStruct(pair.shape, BF16),
                jax.ShapeDtypeStruct(atom_act.shape, BF16),
                jax.ShapeDtypeStruct((tok_rows, agg_width), BF16),
            ),
            in_specs=[in_vmem] * len(args),
            out_specs=(in_vmem,) * 3,
            scratch_shapes=[
                pltpu.VMEM((2, devices * block, tokens), F32),
                pltpu.VMEM((devices, 2, block, tokens), BF16),
                pltpu.VMEM((devices, 2, block, tokens), BF16),
                pltpu.VMEM((devices * block, tokens), F32),
                pltpu.VMEM((devices * block, tokens), F32),
                pltpu.VMEM((devices * block, tokens), F32),
                pltpu.VMEM((devices, block, tokens), BF16),
                pltpu.VMEM((devices, block, tokens), BF16),
                pltpu.VMEM((tok_rows, tokens, channels), F32),
                pltpu.VMEM((slab + 2 * side, 3 * width), BF16),
                pltpu.SemaphoreType.DMA((2,)),
                pltpu.SemaphoreType.DMA((2,)),
                pltpu.SemaphoreType.DMA((2,)),
                pltpu.SemaphoreType.DMA((2,)),
            ],
            compiler_params=pltpu.CompilerParams(
                collective_id=0, has_side_effects=True, vmem_limit_bytes=32 * 1024 * 1024
            ),
            name="triangle_atoms",
        )(*args)
    )


def solution(mesh):
    in_specs = (
        P(("groups", "row"), "col", None),
        P("groups"),
        P(),
        P(),
        P(),
        P(("groups", "row"), None),
        P(("groups", "row"), None),
        P(("groups", "row")),
        P(("groups", "row")),
        P(),
        P(),
        P(),
        P(),
        P(),
        P(),
        P(),
    )
    out_specs = (
        P(("groups", "row"), "col", None),
        P(("groups", "row"), None),
        P(("groups", "row"), None),
    )
    return jax.shard_map(
        per_device, mesh=mesh, in_specs=in_specs, out_specs=out_specs, check_vma=False
    )
```

```python
import functools
import math

import jax
import jax.numpy as jnp
from jax import lax
from jax.experimental import pallas as pl
from jax.experimental.pallas import tpu as pltpu
from jax.sharding import PartitionSpec as P

QUERY_WINDOW = 32
KEYS = 128


EPSILON = 1e-05


def extended(shard, sides, width):
    for axis, dim in sides:
        size, length = (lax.axis_size(axis), shard.shape[dim])
        up = [(i, (i + 1) % size) for i in range(size - 1)]
        down = [(j, i) for i, j in up]
        last = lax.slice_in_dim(shard, length - width, length, axis=dim)
        first = lax.slice_in_dim(shard, 0, width, axis=dim)
        before = lax.ppermute(last, axis, up)
        after = lax.ppermute(first, axis, down)
        shard = jnp.concatenate([before, shard, after], axis=dim)
    return shard


def layer_norm(values, along):
    average = jnp.mean(values, axis=along, keepdims=True)
    centred = values - average
    spread = jnp.mean(centred * centred, axis=along, keepdims=True)
    return centred / jnp.sqrt(spread + EPSILON)


def spread_device(
    pair,
    token_mask,
    tri_in_weight,
    tri_gate_weight,
    tri_out_weight,
    atom_act,
    atom_cond,
    atom_token,
    atom_mask,
    ada_weight,
    qkv_weight,
    bias_weight,
    attn_out_weight,
    ffn_in_weight,
    ffn_out_weight,
    agg_weight,
):
    tok_rows = pair.shape[0]
    col_count = pair.shape[1]
    channels = pair.shape[2]
    row_index = lax.axis_index("row")
    col_index = lax.axis_index("col")
    pair_float = pair.astype(jnp.float32)
    pair_norm = layer_norm(pair_float, 2).astype(jnp.bfloat16)
    row_live = lax.dynamic_slice_in_dim(token_mask, row_index * tok_rows, tok_rows, 0).astype(
        jnp.float32
    )
    col_live = lax.dynamic_slice_in_dim(token_mask, col_index * col_count, col_count, 0).astype(
        jnp.float32
    )
    pair_live = row_live[:, None] * col_live[None, :]
    left_terms = jnp.einsum(
        "ijd,de->eij",
        pair_norm,
        tri_in_weight[:, : 2 * channels],
        preferred_element_type=jnp.float32,
    )
    left = (jax.nn.sigmoid(left_terms[channels:]) * left_terms[:channels] * pair_live).astype(
        jnp.bfloat16
    )
    right_terms = jnp.einsum(
        "ijd,de->eij",
        pair_norm,
        tri_in_weight[:, 2 * channels :],
        preferred_element_type=jnp.float32,
    )
    right = (jax.nn.sigmoid(right_terms[channels:]) * right_terms[:channels] * pair_live).astype(
        jnp.bfloat16
    )
    tri_gate = jax.nn.sigmoid(
        jnp.einsum("ijd,de->ije", pair_norm, tri_gate_weight, preferred_element_type=jnp.float32)
    )
    left_owned, right_owned = (
        lax.all_to_all(left, "row", split_axis=0, concat_axis=1, tiled=True),
        lax.all_to_all(right, "row", split_axis=0, concat_axis=1, tiled=True),
    )
    left_full, right_rows = (
        lax.all_gather(left_owned, "col", axis=2, tiled=True),
        lax.all_gather(right_owned, "col", axis=2, tiled=True),
    )
    right_used = lax.dynamic_slice_in_dim(right_rows, col_index * col_count, col_count, 1)
    tri_sum = jnp.einsum(
        "cik,cjk->cij", left_full, right_used, preferred_element_type=jnp.float32
    ).astype(jnp.bfloat16)
    merged = lax.all_to_all(tri_sum, "row", split_axis=1, concat_axis=0, tiled=True)
    tri_norm = layer_norm(merged.astype(jnp.float32), 0).astype(jnp.bfloat16)
    update = jnp.einsum("dij,de->ije", tri_norm, tri_out_weight, preferred_element_type=jnp.float32)
    pair_out = (pair_float + tri_gate * update).astype(jnp.bfloat16)
    band_width = 3 * tok_rows
    targets = (row_index - 1) * tok_rows + jnp.arange(band_width, dtype=jnp.int32)
    columns = col_index * col_count + jnp.arange(col_count, dtype=jnp.int32)
    selector = (columns[:, None] == targets[None, :]).astype(jnp.bfloat16)
    band_part = jnp.einsum("ijd,jb->ibd", pair_out, selector, preferred_element_type=jnp.float32)
    band = lax.psum(band_part.astype(jnp.bfloat16), "col").astype(jnp.float32)
    band_norm = layer_norm(band, 2).astype(jnp.bfloat16)
    bias_table = jnp.einsum(
        "ibd,dh->ibh", band_norm, bias_weight, preferred_element_type=jnp.float32
    ).astype(jnp.bfloat16)
    slab = atom_act.shape[0]
    window_width = atom_act.shape[1]
    heads = bias_weight.shape[1]
    head_size = window_width // heads
    side = (KEYS - QUERY_WINDOW) // 2
    windows = slab // QUERY_WINDOW
    local_token = atom_token - row_index * tok_rows
    live = atom_mask.astype(jnp.float32)
    token_tag = ((local_token + 1) * atom_mask).astype(jnp.bfloat16)
    ada = jnp.dot(atom_cond, ada_weight, preferred_element_type=jnp.float32)
    atom_inputs = (
        jax.nn.sigmoid(ada[:, :window_width]) * layer_norm(atom_act.astype(jnp.float32), 1)
        + ada[:, window_width:]
    ).astype(jnp.bfloat16)
    projected = jnp.dot(atom_inputs, qkv_weight, preferred_element_type=jnp.float32).astype(
        jnp.bfloat16
    )
    queries = projected[:, :window_width]
    ext_pairs, ext_tag = (
        extended(projected[:, window_width:], (("row", 0),), side),
        extended(token_tag, (("row", 0),), side),
    )
    ext_rows = slab + 2 * side
    ext_position = jnp.arange(ext_rows, dtype=jnp.int32)
    offset = jnp.where(
        ext_position < side, 0, jnp.where(ext_position < side + slab, tok_rows, 2 * tok_rows)
    )
    tag_value = ext_tag.astype(jnp.int32)
    key_valid = tag_value > 0
    band_index = tag_value - 1 + offset
    band_slots = jnp.arange(band_width, dtype=jnp.int32)
    key_onehot = ((band_index[:, None] == band_slots[None, :]) & key_valid[:, None]).astype(
        jnp.bfloat16
    )
    query_onehot = (local_token[:, None] == jnp.arange(tok_rows, dtype=jnp.int32)[None, :]).astype(
        jnp.bfloat16
    )
    query_bias = jnp.einsum(
        "lt,tbh->lbh", query_onehot, bias_table, preferred_element_type=jnp.float32
    ).astype(jnp.bfloat16)
    query_bias = query_bias.reshape(windows, QUERY_WINDOW, band_width, heads)
    key_index = (
        jnp.arange(windows, dtype=jnp.int32)[:, None] * QUERY_WINDOW
        + jnp.arange(KEYS, dtype=jnp.int32)[None, :]
    )
    window_pairs = ext_pairs[key_index]
    window_onehot = key_onehot[key_index]
    window_valid = key_valid[key_index]
    window_bias = jnp.einsum(
        "wlbh,wmb->whlm", query_bias, window_onehot, preferred_element_type=jnp.float32
    )
    query_heads = queries.reshape(windows, QUERY_WINDOW, heads, head_size)
    key_heads = window_pairs[..., :window_width].reshape(windows, KEYS, heads, head_size)
    value_heads = window_pairs[..., window_width:].reshape(windows, KEYS, heads, head_size)
    logit_scores = (
        jnp.einsum("wlhd,wmhd->whlm", query_heads, key_heads, preferred_element_type=jnp.float32)
        / math.sqrt(head_size)
        + window_bias
    )
    logit_scores = jnp.where(window_valid[:, None, None, :], logit_scores, -1e30)
    attn_weights = jax.nn.softmax(logit_scores, axis=-1).astype(jnp.bfloat16)
    attended = (
        jnp.einsum("whlm,wmhd->wlhd", attn_weights, value_heads, preferred_element_type=jnp.float32)
        .reshape(slab, window_width)
        .astype(jnp.bfloat16)
    )
    atom_mid = atom_act.astype(jnp.float32) + jnp.dot(
        attended, attn_out_weight, preferred_element_type=jnp.float32
    )
    atom_norm = layer_norm(atom_mid, 1).astype(jnp.bfloat16)
    expanded = jnp.dot(atom_norm, ffn_in_weight, preferred_element_type=jnp.float32)
    hidden_width = ffn_out_weight.shape[0]
    inner = (jax.nn.silu(expanded[:, :hidden_width]) * expanded[:, hidden_width:]).astype(
        jnp.bfloat16
    )
    atom_out = (
        (atom_mid + jnp.dot(inner, ffn_out_weight, preferred_element_type=jnp.float32))
        * live[:, None]
    ).astype(jnp.bfloat16)
    features = jax.nn.relu(
        jnp.dot(atom_out, agg_weight, preferred_element_type=jnp.float32)
    ).astype(jnp.bfloat16)
    live_onehot = query_onehot * atom_mask.astype(jnp.bfloat16)[:, None]
    token_sums = jnp.einsum("at,ac->tc", live_onehot, features, preferred_element_type=jnp.float32)
    token_counts = jnp.sum(live_onehot.astype(jnp.float32), axis=0)
    token_out = (token_sums / token_counts[:, None]).astype(jnp.bfloat16)
    return (pair_out, atom_out, token_out)


MESH = pl.DeviceIdType.MESH
F32 = jnp.float32
BF16 = jnp.bfloat16


def dot_nn(a, b):
    return lax.dot_general(a, b, (((1,), (0,)), ((), ())), preferred_element_type=F32)


def dot_nt(a, b):
    return lax.dot_general(a, b, (((1,), (1,)), ((), ())), preferred_element_type=F32)


def dot_tn(a, b):
    return lax.dot_general(a, b, (((0,), (0,)), ((), ())), preferred_element_type=F32)


def normed(values, along):
    average = jnp.mean(values, axis=along, keepdims=True)
    centred = values - average
    spread = jnp.mean(centred * centred, axis=along, keepdims=True)
    return centred * lax.rsqrt(spread + EPSILON)


FETCH_ORDER = (0, 2, 1, 3, 6, 9, 5, 7, 8, 10, 4, 11, 12, 13, 14, 15)


def fused_kernel(
    sizes,
    *refs,
):
    count = len(FETCH_ORDER)
    operands, refs = refs[:count], refs[count:]
    (
        pair_out,
        atom_out,
        token_out,
        terms_wide,
        send_terms,
        recv_terms,
        left_wide,
        right_wide,
        sums_wide,
        send_sums,
        recv_sums,
        gate_ref,
        rim,
        send_sem,
        recv_sem,
        rim_send,
        rim_recv,
        fetch_sem,
    ) = refs[: len(refs) - count]
    held = refs[len(refs) - count :]
    fetches = [
        pltpu.make_async_copy(operands[k], held[k], fetch_sem.at[k]) for k in range(count)
    ]
    for k in FETCH_ORDER:
        fetches[k].start()
    (
        pair,
        token_mask,
        tri_in_weight,
        tri_gate_weight,
        tri_out_weight,
        atom_act,
        atom_cond,
        atom_token,
        atom_mask,
        ada_weight,
        qkv_weight,
        bias_weight,
        attn_out_weight,
        ffn_in_weight,
        ffn_out_weight,
        agg_weight,
    ) = held
    devices, tok_rows, tokens, channels, owned, slab, heads = sizes
    block = tok_rows * owned
    side = (KEYS - QUERY_WINDOW) // 2
    ext = slab + 2 * side
    group = lax.axis_index("groups")
    me = lax.axis_index("row")
    col = lax.axis_index("col")

    barrier = pltpu.get_barrier_semaphore()

    def greet(step, carry):
        peer = lax.rem(me + step, devices)
        pl.semaphore_signal(barrier, inc=1, device_id=(group, peer, col), device_id_type=MESH)
        return carry

    lax.fori_loop(1, devices, greet, 0)

    for k in (0, 2, 1, 3):
        fetches[k].wait()
    mask_row = token_mask[...].astype(F32)
    lane = lax.broadcasted_iota(jnp.int32, (1, tokens), 1)
    in_weight = tri_in_weight[...].T
    for i in range(tok_rows):
        norm = normed(pair[i].astype(F32), 1).astype(BF16)
        row_mask = jnp.sum(jnp.where(lane == me * tok_rows + i, mask_row, 0.0), axis=1, keepdims=True)
        both = row_mask * mask_row
        terms = dot_nt(in_weight, norm)
        for part in range(2):
            base = part * 2 * channels
            value = (
                jax.nn.sigmoid(terms[base + channels : base + 2 * channels])
                * terms[base : base + channels]
                * both
            )
            for c in range(owned):
                terms_wide[part, pl.ds(i * owned + c, devices, stride=block), :] = value[
                    c * devices : (c + 1) * devices
                ]
        gate_ref[i] = jax.nn.sigmoid(dot_nn(norm, tri_gate_weight[...]))
    for part in range(2):
        send_terms[:, part] = terms_wide[part].reshape(devices, block, tokens).astype(BF16)

    pl.semaphore_wait(barrier, devices - 1)

    def terms_copy(peer):
        return pltpu.make_async_remote_copy(
            src_ref=send_terms.at[peer],
            dst_ref=recv_terms.at[me],
            send_sem=send_sem.at[0],
            recv_sem=recv_sem.at[0],
            device_id=(group, peer, col),
            device_id_type=MESH,
        )

    def send_first(step, carry):
        terms_copy(lax.rem(me + step, devices)).start()
        return carry

    lax.fori_loop(1, devices, send_first, 0)
    recv_terms[me] = send_terms[me]

    for k in (6, 9, 5, 7, 8, 10):
        fetches[k].wait()
    token_row = atom_token[...] - me * tok_rows
    live_row = atom_mask[...]
    wide = (channels, slab)
    token_col = jnp.broadcast_to(token_row.astype(F32), wide).T
    live_col = jnp.broadcast_to(live_row.astype(F32), wide).T
    act = atom_act[...].astype(F32)
    ada = dot_nn(atom_cond[...], ada_weight[...])
    width = act.shape[1]
    atom_inputs = (jax.nn.sigmoid(ada[:, :width]) * normed(act, 1) + ada[:, width:]).astype(BF16)
    projected = dot_nn(atom_inputs, qkv_weight[...]).astype(BF16)
    rim[side : side + slab, : 2 * width] = projected[:, width:]
    rim[side : side + slab, 2 * width :] = ((token_col + 1.0) * live_col).astype(BF16)

    up = pltpu.make_async_remote_copy(
        src_ref=rim.at[pl.ds(slab, side)],
        dst_ref=rim.at[pl.ds(0, side)],
        send_sem=rim_send.at[0],
        recv_sem=rim_recv.at[0],
        device_id=(group, lax.rem(me + 1, devices), col),
        device_id_type=MESH,
    )
    down = pltpu.make_async_remote_copy(
        src_ref=rim.at[pl.ds(side, side)],
        dst_ref=rim.at[pl.ds(side + slab, side)],
        send_sem=rim_send.at[1],
        recv_sem=rim_recv.at[1],
        device_id=(group, lax.rem(me + devices - 1, devices), col),
        device_id_type=MESH,
    )

    @pl.when(me < devices - 1)
    def _():
        up.start()

    @pl.when(me > 0)
    def _():
        down.start()

    @pl.when(me == 0)
    def _():
        rim[:side] = jnp.zeros((side, rim.shape[1]), BF16)

    @pl.when(me == devices - 1)
    def _():
        rim[side + slab :] = jnp.zeros((side, rim.shape[1]), BF16)

    others = pl.ds(0, devices - 1)
    pltpu.make_async_copy(send_terms.at[others], recv_terms.at[others], recv_sem.at[0]).wait()
    left_wide[...] = recv_terms[:, 0].reshape(devices * block, tokens).astype(F32)
    right_wide[...] = recv_terms[:, 1].reshape(devices * block, tokens).astype(F32)
    for c in range(owned):
        rows = pl.ds(c, tokens, stride=owned)
        sums_wide[rows, :] = dot_nt(
            left_wide[rows, :].astype(BF16), right_wide[rows, :].astype(BF16)
        )
    send_sums[...] = sums_wide[...].reshape(devices, block, tokens).astype(BF16)

    def sums_copy(peer):
        return pltpu.make_async_remote_copy(
            src_ref=send_sums.at[peer],
            dst_ref=recv_sums.at[me],
            send_sem=send_sem.at[1],
            recv_sem=recv_sem.at[1],
            device_id=(group, peer, col),
            device_id_type=MESH,
        )

    def send_second(step, carry):
        sums_copy(lax.rem(me + step, devices)).start()
        return carry

    lax.fori_loop(1, devices, send_second, 0)
    recv_sums[me] = send_sums[me]

    @pl.when(me > 0)
    def _():
        up.wait_recv()

    @pl.when(me < devices - 1)
    def _():
        down.wait_recv()

    head_size = width // heads
    keys = rim[:, :width]
    values = rim[:, width : 2 * width]
    tag = rim[:, 2 * width :].astype(F32)
    head_lane = lax.broadcasted_iota(jnp.int32, (slab, width), 1) // head_size
    queries = projected[:, :width].astype(F32)
    split_queries = jnp.concatenate(
        [jnp.where(head_lane == h, queries, 0.0) for h in range(heads)], axis=0
    ).astype(BF16)
    raw_scores = dot_nt(split_queries, keys) * (1.0 / math.sqrt(head_size))
    band = 4 * tok_rows
    dead_lane = tok_rows * band
    ext_row = lax.broadcasted_iota(jnp.int32, (ext, channels), 0)
    ext_lane = lax.broadcasted_iota(jnp.int32, (ext, channels), 1)
    offset = jnp.where(
        ext_row < side, 0, jnp.where(ext_row < side + slab, tok_rows, 2 * tok_rows)
    )
    band_index = tag.astype(jnp.int32) - 1 + offset
    slot = lax.rem(ext_lane, band)
    alive = tag > 0.0
    key_map = jnp.where(
        ext_lane < dead_lane,
        jnp.where(alive & (band_index == slot), 1.0, 0.0),
        jnp.where(alive, 0.0, 1.0),
    ).astype(BF16)
    query_lane = lax.broadcasted_iota(jnp.int32, (slab, channels), 1)
    query_map = jnp.where(
        (query_lane // band == token_col.astype(jnp.int32)) | (query_lane == dead_lane), 1.0, 0.0
    )
    score_row = lax.broadcasted_iota(jnp.int32, (slab, ext), 0) // QUERY_WINDOW * QUERY_WINDOW
    score_lane = lax.broadcasted_iota(jnp.int32, (slab, ext), 1)
    in_window = (score_lane >= score_row) & (score_lane < score_row + KEYS)

    for k in (4, 11, 12, 13, 14, 15):
        fetches[k].wait()
    pltpu.make_async_copy(send_sums.at[others], recv_sums.at[others], recv_sem.at[1]).wait()
    sums_wide[...] = recv_sums[...].reshape(devices * block, tokens).astype(F32)
    band_row = lax.broadcasted_iota(jnp.int32, (band, tokens), 0)
    band_lane = lax.broadcasted_iota(jnp.int32, (band, tokens), 1)
    selector = jnp.where(
        (band_lane == (me - 1) * tok_rows + band_row) & (band_row < 3 * tok_rows), 1.0, 0.0
    ).astype(BF16)
    bands = []
    for i in range(tok_rows):
        merged = jnp.concatenate(
            [
                sums_wide[pl.ds(i * owned + c, devices, stride=block), :]
                for c in range(owned)
            ],
            axis=0,
        )
        tri_norm = normed(merged, 0).T.astype(BF16)
        update = dot_nn(tri_norm, tri_out_weight[...])
        updated = (pair[i].astype(F32) + gate_ref[i] * update).astype(BF16)
        pair_out[i] = updated
        bands.append(dot_nn(selector, updated))
    bands.append(jnp.zeros((channels - tok_rows * band, channels), F32))
    band_norm = normed(jnp.concatenate(bands, axis=0), 1).astype(BF16)
    table = dot_nt(bias_weight[...], band_norm).astype(BF16).astype(F32)
    table_lane = lax.broadcasted_iota(jnp.int32, table.shape, 1)
    table = jnp.where(table_lane == dead_lane, -1e30, table)
    bias_rows = jnp.concatenate(
        [query_map * table[h : h + 1] for h in range(heads)], axis=0
    ).astype(BF16)
    scores = raw_scores + dot_nt(bias_rows, key_map)
    scores = jnp.where(jnp.concatenate([in_window] * heads, axis=0), scores, -1e30)
    scores = jnp.exp(scores - jnp.max(scores, axis=1, keepdims=True))
    weights = (scores / jnp.sum(scores, axis=1, keepdims=True)).astype(BF16)
    mixed = dot_nn(weights, values)
    attended = jnp.zeros((slab, width), F32)
    for h in range(heads):
        attended = jnp.where(head_lane == h, mixed[h * slab : (h + 1) * slab], attended)
    atom_mid = act + dot_nn(attended.astype(BF16), attn_out_weight[...])
    expanded = dot_nn(normed(atom_mid, 1).astype(BF16), ffn_in_weight[...])
    hidden = ffn_out_weight.shape[0]
    up_part, gate_part = expanded[:, hidden:], expanded[:, :hidden]
    inner = (gate_part * jax.nn.sigmoid(gate_part) * up_part).astype(BF16)
    result = ((atom_mid + dot_nn(inner, ffn_out_weight[...])) * live_col).astype(BF16)
    atom_out[...] = result
    features = jnp.maximum(dot_nn(result, agg_weight[...]), 0.0).astype(BF16)
    owner_row = lax.broadcasted_iota(jnp.int32, (tok_rows, slab), 0)
    owner = jnp.where((owner_row == token_row) & (live_row > 0), 1.0, 0.0)
    counts = jnp.sum(owner, axis=1, keepdims=True)
    token_out[...] = (dot_nn(owner.astype(BF16), features) / counts).astype(BF16)

    pltpu.make_async_copy(send_terms.at[others], recv_terms.at[others], send_sem.at[0]).wait()
    pltpu.make_async_copy(send_sums.at[others], recv_sums.at[others], send_sem.at[1]).wait()

    @pl.when(me < devices - 1)
    def _():
        up.wait_send()

    @pl.when(me > 0)
    def _():
        down.wait_send()


def per_device(*args):
    pair, token_mask, atom_act, atom_token = args[0], args[1], args[5], args[7]
    tok_rows, tokens, channels = pair.shape
    slab, width = atom_act.shape
    heads = args[11].shape[1]
    devices = lax.axis_size("row")
    owned = channels // devices
    block = tok_rows * owned
    fits = (
        lax.axis_size("col") == 1
        and owned * devices == channels
        and block % 16 == 0
        and slab % QUERY_WINDOW == 0
        and devices % 8 == 0
        and width == channels
        and 4 * tok_rows % 16 == 0
        and 4 * tok_rows * tok_rows < channels
        and slab >= (KEYS - QUERY_WINDOW) // 2
    )
    if not fits:
        return spread_device(*args)
    side = (KEYS - QUERY_WINDOW) // 2
    args = list(args)
    for k in (1, 7, 8):
        args[k] = args[k].reshape(1, -1)
    args[11] = args[11].T
    agg_width = args[15].shape[1]
    sizes = (devices, tok_rows, tokens, channels, owned, slab, heads)
    in_vmem = pl.BlockSpec(memory_space=pltpu.VMEM)
    in_hbm = pl.BlockSpec(memory_space=pltpu.HBM)
    return tuple(
        pl.pallas_call(
            functools.partial(fused_kernel, sizes),
            out_shape=(
                jax.ShapeDtypeStruct(pair.shape, BF16),
                jax.ShapeDtypeStruct(atom_act.shape, BF16),
                jax.ShapeDtypeStruct((tok_rows, agg_width), BF16),
            ),
            in_specs=[in_hbm] * len(args),
            out_specs=(in_vmem,) * 3,
            scratch_shapes=[
                pltpu.VMEM((2, devices * block, tokens), F32),
                pltpu.VMEM((devices, 2, block, tokens), BF16),
                pltpu.VMEM((devices, 2, block, tokens), BF16),
                pltpu.VMEM((devices * block, tokens), F32),
                pltpu.VMEM((devices * block, tokens), F32),
                pltpu.VMEM((devices * block, tokens), F32),
                pltpu.VMEM((devices, block, tokens), BF16),
                pltpu.VMEM((devices, block, tokens), BF16),
                pltpu.VMEM((tok_rows, tokens, channels), F32),
                pltpu.VMEM((slab + 2 * side, 3 * width), BF16),
                pltpu.SemaphoreType.DMA((2,)),
                pltpu.SemaphoreType.DMA((2,)),
                pltpu.SemaphoreType.DMA((2,)),
                pltpu.SemaphoreType.DMA((2,)),
                pltpu.SemaphoreType.DMA((len(args),)),
                *[pltpu.VMEM(a.shape, a.dtype) for a in args],
            ],
            compiler_params=pltpu.CompilerParams(
                collective_id=0, has_side_effects=True, vmem_limit_bytes=60 * 1024 * 1024
            ),
            name="triangle_atoms",
        )(*args)
    )


def solution(mesh):
    in_specs = (
        P(("groups", "row"), "col", None),
        P("groups"),
        P(),
        P(),
        P(),
        P(("groups", "row"), None),
        P(("groups", "row"), None),
        P(("groups", "row")),
        P(("groups", "row")),
        P(),
        P(),
        P(),
        P(),
        P(),
        P(),
        P(),
    )
    out_specs = (
        P(("groups", "row"), "col", None),
        P(("groups", "row"), None),
        P(("groups", "row"), None),
    )
    return jax.shard_map(
        per_device, mesh=mesh, in_specs=in_specs, out_specs=out_specs, check_vma=False
    )
```

```python
import functools
import math

import jax
import jax.numpy as jnp
from jax import lax
from jax.experimental import pallas as pl
from jax.experimental.pallas import tpu as pltpu
from jax.sharding import PartitionSpec as P

QUERY_WINDOW = 32
KEYS = 128


EPSILON = 1e-05


def extended(shard, sides, width):
    for axis, dim in sides:
        size, length = (lax.axis_size(axis), shard.shape[dim])
        up = [(i, (i + 1) % size) for i in range(size - 1)]
        down = [(j, i) for i, j in up]
        last = lax.slice_in_dim(shard, length - width, length, axis=dim)
        first = lax.slice_in_dim(shard, 0, width, axis=dim)
        before = lax.ppermute(last, axis, up)
        after = lax.ppermute(first, axis, down)
        shard = jnp.concatenate([before, shard, after], axis=dim)
    return shard


def layer_norm(values, along):
    average = jnp.mean(values, axis=along, keepdims=True)
    centred = values - average
    spread = jnp.mean(centred * centred, axis=along, keepdims=True)
    return centred / jnp.sqrt(spread + EPSILON)


def spread_device(
    pair,
    token_mask,
    tri_in_weight,
    tri_gate_weight,
    tri_out_weight,
    atom_act,
    atom_cond,
    atom_token,
    atom_mask,
    ada_weight,
    qkv_weight,
    bias_weight,
    attn_out_weight,
    ffn_in_weight,
    ffn_out_weight,
    agg_weight,
):
    tok_rows = pair.shape[0]
    col_count = pair.shape[1]
    channels = pair.shape[2]
    row_index = lax.axis_index("row")
    col_index = lax.axis_index("col")
    pair_float = pair.astype(jnp.float32)
    pair_norm = layer_norm(pair_float, 2).astype(jnp.bfloat16)
    row_live = lax.dynamic_slice_in_dim(token_mask, row_index * tok_rows, tok_rows, 0).astype(
        jnp.float32
    )
    col_live = lax.dynamic_slice_in_dim(token_mask, col_index * col_count, col_count, 0).astype(
        jnp.float32
    )
    pair_live = row_live[:, None] * col_live[None, :]
    left_terms = jnp.einsum(
        "ijd,de->eij",
        pair_norm,
        tri_in_weight[:, : 2 * channels],
        preferred_element_type=jnp.float32,
    )
    left = (jax.nn.sigmoid(left_terms[channels:]) * left_terms[:channels] * pair_live).astype(
        jnp.bfloat16
    )
    right_terms = jnp.einsum(
        "ijd,de->eij",
        pair_norm,
        tri_in_weight[:, 2 * channels :],
        preferred_element_type=jnp.float32,
    )
    right = (jax.nn.sigmoid(right_terms[channels:]) * right_terms[:channels] * pair_live).astype(
        jnp.bfloat16
    )
    tri_gate = jax.nn.sigmoid(
        jnp.einsum("ijd,de->ije", pair_norm, tri_gate_weight, preferred_element_type=jnp.float32)
    )
    left_owned, right_owned = (
        lax.all_to_all(left, "row", split_axis=0, concat_axis=1, tiled=True),
        lax.all_to_all(right, "row", split_axis=0, concat_axis=1, tiled=True),
    )
    left_full, right_rows = (
        lax.all_gather(left_owned, "col", axis=2, tiled=True),
        lax.all_gather(right_owned, "col", axis=2, tiled=True),
    )
    right_used = lax.dynamic_slice_in_dim(right_rows, col_index * col_count, col_count, 1)
    tri_sum = jnp.einsum(
        "cik,cjk->cij", left_full, right_used, preferred_element_type=jnp.float32
    ).astype(jnp.bfloat16)
    merged = lax.all_to_all(tri_sum, "row", split_axis=1, concat_axis=0, tiled=True)
    tri_norm = layer_norm(merged.astype(jnp.float32), 0).astype(jnp.bfloat16)
    update = jnp.einsum("dij,de->ije", tri_norm, tri_out_weight, preferred_element_type=jnp.float32)
    pair_out = (pair_float + tri_gate * update).astype(jnp.bfloat16)
    band_width = 3 * tok_rows
    targets = (row_index - 1) * tok_rows + jnp.arange(band_width, dtype=jnp.int32)
    columns = col_index * col_count + jnp.arange(col_count, dtype=jnp.int32)
    selector = (columns[:, None] == targets[None, :]).astype(jnp.bfloat16)
    band_part = jnp.einsum("ijd,jb->ibd", pair_out, selector, preferred_element_type=jnp.float32)
    band = lax.psum(band_part.astype(jnp.bfloat16), "col").astype(jnp.float32)
    band_norm = layer_norm(band, 2).astype(jnp.bfloat16)
    bias_table = jnp.einsum(
        "ibd,dh->ibh", band_norm, bias_weight, preferred_element_type=jnp.float32
    ).astype(jnp.bfloat16)
    slab = atom_act.shape[0]
    window_width = atom_act.shape[1]
    heads = bias_weight.shape[1]
    head_size = window_width // heads
    side = (KEYS - QUERY_WINDOW) // 2
    windows = slab // QUERY_WINDOW
    local_token = atom_token - row_index * tok_rows
    live = atom_mask.astype(jnp.float32)
    token_tag = ((local_token + 1) * atom_mask).astype(jnp.bfloat16)
    ada = jnp.dot(atom_cond, ada_weight, preferred_element_type=jnp.float32)
    atom_inputs = (
        jax.nn.sigmoid(ada[:, :window_width]) * layer_norm(atom_act.astype(jnp.float32), 1)
        + ada[:, window_width:]
    ).astype(jnp.bfloat16)
    projected = jnp.dot(atom_inputs, qkv_weight, preferred_element_type=jnp.float32).astype(
        jnp.bfloat16
    )
    queries = projected[:, :window_width]
    ext_pairs, ext_tag = (
        extended(projected[:, window_width:], (("row", 0),), side),
        extended(token_tag, (("row", 0),), side),
    )
    ext_rows = slab + 2 * side
    ext_position = jnp.arange(ext_rows, dtype=jnp.int32)
    offset = jnp.where(
        ext_position < side, 0, jnp.where(ext_position < side + slab, tok_rows, 2 * tok_rows)
    )
    tag_value = ext_tag.astype(jnp.int32)
    key_valid = tag_value > 0
    band_index = tag_value - 1 + offset
    band_slots = jnp.arange(band_width, dtype=jnp.int32)
    key_onehot = ((band_index[:, None] == band_slots[None, :]) & key_valid[:, None]).astype(
        jnp.bfloat16
    )
    query_onehot = (local_token[:, None] == jnp.arange(tok_rows, dtype=jnp.int32)[None, :]).astype(
        jnp.bfloat16
    )
    query_bias = jnp.einsum(
        "lt,tbh->lbh", query_onehot, bias_table, preferred_element_type=jnp.float32
    ).astype(jnp.bfloat16)
    query_bias = query_bias.reshape(windows, QUERY_WINDOW, band_width, heads)
    key_index = (
        jnp.arange(windows, dtype=jnp.int32)[:, None] * QUERY_WINDOW
        + jnp.arange(KEYS, dtype=jnp.int32)[None, :]
    )
    window_pairs = ext_pairs[key_index]
    window_onehot = key_onehot[key_index]
    window_valid = key_valid[key_index]
    window_bias = jnp.einsum(
        "wlbh,wmb->whlm", query_bias, window_onehot, preferred_element_type=jnp.float32
    )
    query_heads = queries.reshape(windows, QUERY_WINDOW, heads, head_size)
    key_heads = window_pairs[..., :window_width].reshape(windows, KEYS, heads, head_size)
    value_heads = window_pairs[..., window_width:].reshape(windows, KEYS, heads, head_size)
    logit_scores = (
        jnp.einsum("wlhd,wmhd->whlm", query_heads, key_heads, preferred_element_type=jnp.float32)
        / math.sqrt(head_size)
        + window_bias
    )
    logit_scores = jnp.where(window_valid[:, None, None, :], logit_scores, -1e30)
    attn_weights = jax.nn.softmax(logit_scores, axis=-1).astype(jnp.bfloat16)
    attended = (
        jnp.einsum("whlm,wmhd->wlhd", attn_weights, value_heads, preferred_element_type=jnp.float32)
        .reshape(slab, window_width)
        .astype(jnp.bfloat16)
    )
    atom_mid = atom_act.astype(jnp.float32) + jnp.dot(
        attended, attn_out_weight, preferred_element_type=jnp.float32
    )
    atom_norm = layer_norm(atom_mid, 1).astype(jnp.bfloat16)
    expanded = jnp.dot(atom_norm, ffn_in_weight, preferred_element_type=jnp.float32)
    hidden_width = ffn_out_weight.shape[0]
    inner = (jax.nn.silu(expanded[:, :hidden_width]) * expanded[:, hidden_width:]).astype(
        jnp.bfloat16
    )
    atom_out = (
        (atom_mid + jnp.dot(inner, ffn_out_weight, preferred_element_type=jnp.float32))
        * live[:, None]
    ).astype(jnp.bfloat16)
    features = jax.nn.relu(
        jnp.dot(atom_out, agg_weight, preferred_element_type=jnp.float32)
    ).astype(jnp.bfloat16)
    live_onehot = query_onehot * atom_mask.astype(jnp.bfloat16)[:, None]
    token_sums = jnp.einsum("at,ac->tc", live_onehot, features, preferred_element_type=jnp.float32)
    token_counts = jnp.sum(live_onehot.astype(jnp.float32), axis=0)
    token_out = (token_sums / token_counts[:, None]).astype(jnp.bfloat16)
    return (pair_out, atom_out, token_out)


MESH = pl.DeviceIdType.MESH
F32 = jnp.float32
BF16 = jnp.bfloat16


def dot_nn(a, b):
    return lax.dot_general(a, b, (((1,), (0,)), ((), ())), preferred_element_type=F32)


def dot_nt(a, b):
    return lax.dot_general(a, b, (((1,), (1,)), ((), ())), preferred_element_type=F32)


def dot_tn(a, b):
    return lax.dot_general(a, b, (((0,), (0,)), ((), ())), preferred_element_type=F32)


def normed(values, along):
    average = jnp.mean(values, axis=along, keepdims=True)
    centred = values - average
    spread = jnp.mean(centred * centred, axis=along, keepdims=True)
    return centred * lax.rsqrt(spread + EPSILON)


FETCH_ORDER = (0, 2, 1, 3, 6, 9, 5, 7, 8, 10, 4, 11, 12, 13, 14, 15)


def fused_kernel(
    sizes,
    *refs,
):
    count = len(FETCH_ORDER)
    operands, refs = refs[:count], refs[count:]
    (
        pair_out,
        atom_out,
        token_out,
        terms_wide,
        send_terms,
        recv_terms,
        left_wide,
        right_wide,
        sums_wide,
        send_sums,
        recv_sums,
        gate_ref,
        rim,
        send_sem,
        recv_sem,
        rim_send,
        rim_recv,
        fetch_sem,
    ) = refs[: len(refs) - count]
    held = refs[len(refs) - count :]
    fetches = [
        pltpu.make_async_copy(operands[k], held[k], fetch_sem.at[k]) for k in range(count)
    ]
    for k in FETCH_ORDER:
        fetches[k].start()
    (
        pair,
        token_mask,
        tri_in_weight,
        tri_gate_weight,
        tri_out_weight,
        atom_act,
        atom_cond,
        atom_token,
        atom_mask,
        ada_weight,
        qkv_weight,
        bias_weight,
        attn_out_weight,
        ffn_in_weight,
        ffn_out_weight,
        agg_weight,
    ) = held
    devices, tok_rows, tokens, channels, owned, slab, heads = sizes
    block = tok_rows * owned
    side = (KEYS - QUERY_WINDOW) // 2
    ext = slab + 2 * side
    group = lax.axis_index("groups")
    me = lax.axis_index("row")
    col = lax.axis_index("col")

    barrier = pltpu.get_barrier_semaphore()

    def greet(step, carry):
        peer = lax.rem(me + step, devices)
        pl.semaphore_signal(barrier, inc=1, device_id=(group, peer, col), device_id_type=MESH)
        return carry

    lax.fori_loop(1, devices, greet, 0)

    for k in (0, 2, 1, 3):
        fetches[k].wait()
    mask_row = token_mask[...].astype(F32)
    lane = lax.broadcasted_iota(jnp.int32, (1, tokens), 1)
    in_weight = tri_in_weight[...].T
    for i in range(tok_rows):
        norm = normed(pair[i].astype(F32), 1).astype(BF16)
        row_mask = jnp.sum(jnp.where(lane == me * tok_rows + i, mask_row, 0.0), axis=1, keepdims=True)
        both = row_mask * mask_row
        terms = dot_nt(in_weight, norm)
        for part in range(2):
            base = part * 2 * channels
            value = (
                jax.nn.sigmoid(terms[base + channels : base + 2 * channels])
                * terms[base : base + channels]
                * both
            )
            for c in range(owned):
                terms_wide[part, pl.ds(i * owned + c, devices, stride=block), :] = value[
                    c * devices : (c + 1) * devices
                ]
        gate_ref[i] = jax.nn.sigmoid(dot_nn(norm, tri_gate_weight[...]))
    for part in range(2):
        send_terms[:, part] = terms_wide[part].reshape(devices, block, tokens).astype(BF16)

    pl.semaphore_wait(barrier, devices - 1)

    def terms_copy(peer):
        return pltpu.make_async_remote_copy(
            src_ref=send_terms.at[peer],
            dst_ref=recv_terms.at[me],
            send_sem=send_sem.at[0],
            recv_sem=recv_sem.at[0],
            device_id=(group, peer, col),
            device_id_type=MESH,
        )

    def send_first(step, carry):
        terms_copy(lax.rem(me + step, devices)).start()
        return carry

    lax.fori_loop(1, devices, send_first, 0)
    recv_terms[me] = send_terms[me]

    for k in (6, 9, 5, 7, 8, 10):
        fetches[k].wait()
    token_row = atom_token[...] - me * tok_rows
    live_row = atom_mask[...]
    wide = (channels, slab)
    token_col = jnp.broadcast_to(token_row.astype(F32), wide).T
    live_col = jnp.broadcast_to(live_row.astype(F32), wide).T
    act = atom_act[...].astype(F32)
    ada = dot_nn(atom_cond[...], ada_weight[...])
    width = act.shape[1]
    atom_inputs = (jax.nn.sigmoid(ada[:, :width]) * normed(act, 1) + ada[:, width:]).astype(BF16)
    projected = dot_nn(atom_inputs, qkv_weight[...]).astype(BF16)
    rim[side : side + slab, : 2 * width] = projected[:, width:]
    rim[side : side + slab, 2 * width :] = ((token_col + 1.0) * live_col).astype(BF16)

    up = pltpu.make_async_remote_copy(
        src_ref=rim.at[pl.ds(slab, side)],
        dst_ref=rim.at[pl.ds(0, side)],
        send_sem=rim_send.at[0],
        recv_sem=rim_recv.at[0],
        device_id=(group, lax.rem(me + 1, devices), col),
        device_id_type=MESH,
    )
    down = pltpu.make_async_remote_copy(
        src_ref=rim.at[pl.ds(side, side)],
        dst_ref=rim.at[pl.ds(side + slab, side)],
        send_sem=rim_send.at[1],
        recv_sem=rim_recv.at[1],
        device_id=(group, lax.rem(me + devices - 1, devices), col),
        device_id_type=MESH,
    )

    @pl.when(me < devices - 1)
    def _():
        up.start()

    @pl.when(me > 0)
    def _():
        down.start()

    @pl.when(me == 0)
    def _():
        rim[:side] = jnp.zeros((side, rim.shape[1]), BF16)

    @pl.when(me == devices - 1)
    def _():
        rim[side + slab :] = jnp.zeros((side, rim.shape[1]), BF16)

    others = pl.ds(0, devices - 1)
    pltpu.make_async_copy(send_terms.at[others], recv_terms.at[others], recv_sem.at[0]).wait()
    left_wide[...] = recv_terms[:, 0].reshape(devices * block, tokens).astype(F32)
    right_wide[...] = recv_terms[:, 1].reshape(devices * block, tokens).astype(F32)
    for c in range(owned):
        rows = pl.ds(c, tokens, stride=owned)
        sums_wide[rows, :] = dot_nt(
            left_wide[rows, :].astype(BF16), right_wide[rows, :].astype(BF16)
        )
    send_sums[...] = sums_wide[...].reshape(devices, block, tokens).astype(BF16)

    def sums_copy(peer):
        return pltpu.make_async_remote_copy(
            src_ref=send_sums.at[peer],
            dst_ref=recv_sums.at[me],
            send_sem=send_sem.at[1],
            recv_sem=recv_sem.at[1],
            device_id=(group, peer, col),
            device_id_type=MESH,
        )

    def send_second(step, carry):
        sums_copy(lax.rem(me + step, devices)).start()
        return carry

    lax.fori_loop(1, devices, send_second, 0)
    recv_sums[me] = send_sums[me]

    @pl.when(me > 0)
    def _():
        up.wait_recv()

    @pl.when(me < devices - 1)
    def _():
        down.wait_recv()

    head_size = width // heads
    keys = rim[:, :width]
    values = rim[:, width : 2 * width]
    tag = rim[:, 2 * width :].astype(F32)
    head_lane = lax.broadcasted_iota(jnp.int32, (slab, width), 1) // head_size
    queries = projected[:, :width].astype(F32)
    split_queries = jnp.concatenate(
        [jnp.where(head_lane == h, queries, 0.0) for h in range(heads)], axis=0
    ).astype(BF16)
    raw_scores = dot_nt(split_queries, keys) * (1.0 / math.sqrt(head_size))
    band = 4 * tok_rows
    dead_lane = tok_rows * band
    ext_row = lax.broadcasted_iota(jnp.int32, (ext, channels), 0)
    ext_lane = lax.broadcasted_iota(jnp.int32, (ext, channels), 1)
    offset = jnp.where(
        ext_row < side, 0, jnp.where(ext_row < side + slab, tok_rows, 2 * tok_rows)
    )
    band_index = tag.astype(jnp.int32) - 1 + offset
    slot = lax.rem(ext_lane, band)
    alive = tag > 0.0
    key_map = jnp.where(
        ext_lane < dead_lane,
        jnp.where(alive & (band_index == slot), 1.0, 0.0),
        jnp.where(alive, 0.0, 1.0),
    ).astype(BF16)
    query_lane = lax.broadcasted_iota(jnp.int32, (slab, channels), 1)
    query_map = jnp.where(
        (query_lane // band == token_col.astype(jnp.int32)) | (query_lane == dead_lane), 1.0, 0.0
    )
    score_row = lax.broadcasted_iota(jnp.int32, (slab, ext), 0) // QUERY_WINDOW * QUERY_WINDOW
    score_lane = lax.broadcasted_iota(jnp.int32, (slab, ext), 1)
    in_window = (score_lane >= score_row) & (score_lane < score_row + KEYS)

    for k in (4, 11, 12, 13, 14, 15):
        fetches[k].wait()
    pltpu.make_async_copy(send_sums.at[others], recv_sums.at[others], recv_sem.at[1]).wait()
    sums_wide[...] = recv_sums[...].reshape(devices * block, tokens).astype(F32)
    band_row = lax.broadcasted_iota(jnp.int32, (band, tokens), 0)
    band_lane = lax.broadcasted_iota(jnp.int32, (band, tokens), 1)
    selector = jnp.where(
        (band_lane == (me - 1) * tok_rows + band_row) & (band_row < 3 * tok_rows), 1.0, 0.0
    ).astype(BF16)
    bands = []
    for i in range(tok_rows):
        merged = jnp.concatenate(
            [
                sums_wide[pl.ds(i * owned + c, devices, stride=block), :]
                for c in range(owned)
            ],
            axis=0,
        )
        tri_norm = normed(merged, 0).T.astype(BF16)
        update = dot_nn(tri_norm, tri_out_weight[...])
        updated = (pair[i].astype(F32) + gate_ref[i] * update).astype(BF16)
        pair_out[i] = updated
        bands.append(dot_nn(selector, updated))
    bands.append(jnp.zeros((channels - tok_rows * band, channels), F32))
    band_norm = normed(jnp.concatenate(bands, axis=0), 1).astype(BF16)
    table = dot_nt(bias_weight[...], band_norm).astype(BF16).astype(F32)
    table_lane = lax.broadcasted_iota(jnp.int32, table.shape, 1)
    table = jnp.where(table_lane == dead_lane, -1e30, table)
    bias_rows = jnp.concatenate(
        [query_map * table[h : h + 1] for h in range(heads)], axis=0
    ).astype(BF16)
    scores = raw_scores + dot_nt(bias_rows, key_map)
    scores = jnp.where(jnp.concatenate([in_window] * heads, axis=0), scores, -1e30)
    scores = jnp.exp(scores - jnp.max(scores, axis=1, keepdims=True))
    weights = (scores / jnp.sum(scores, axis=1, keepdims=True)).astype(BF16)
    mixed = dot_nn(weights, values)
    attended = jnp.zeros((slab, width), F32)
    for h in range(heads):
        attended = jnp.where(head_lane == h, mixed[h * slab : (h + 1) * slab], attended)
    atom_mid = act + dot_nn(attended.astype(BF16), attn_out_weight[...])
    expanded = dot_nn(normed(atom_mid, 1).astype(BF16), ffn_in_weight[...])
    hidden = ffn_out_weight.shape[0]
    up_part, gate_part = expanded[:, hidden:], expanded[:, :hidden]
    inner = (gate_part * jax.nn.sigmoid(gate_part) * up_part).astype(BF16)
    result = ((atom_mid + dot_nn(inner, ffn_out_weight[...])) * live_col).astype(BF16)
    atom_out[...] = result
    features = jnp.maximum(dot_nn(result, agg_weight[...]), 0.0).astype(BF16)
    owner_row = lax.broadcasted_iota(jnp.int32, (tok_rows, slab), 0)
    owner = jnp.where((owner_row == token_row) & (live_row > 0), 1.0, 0.0)
    counts = jnp.sum(owner, axis=1, keepdims=True)
    token_out[...] = (dot_nn(owner.astype(BF16), features) / counts).astype(BF16)

    pltpu.make_async_copy(send_terms.at[others], recv_terms.at[others], send_sem.at[0]).wait()
    pltpu.make_async_copy(send_sums.at[others], recv_sums.at[others], send_sem.at[1]).wait()

    @pl.when(me < devices - 1)
    def _():
        up.wait_send()

    @pl.when(me > 0)
    def _():
        down.wait_send()


def per_device(*args):
    pair, token_mask, atom_act, atom_token = args[0], args[1], args[5], args[7]
    tok_rows, tokens, channels = pair.shape
    slab, width = atom_act.shape
    heads = args[11].shape[1]
    devices = lax.axis_size("row")
    owned = channels // devices
    block = tok_rows * owned
    fits = (
        lax.axis_size("col") == 1
        and owned * devices == channels
        and block % 16 == 0
        and slab % QUERY_WINDOW == 0
        and devices % 8 == 0
        and width == channels
        and 4 * tok_rows % 16 == 0
        and 4 * tok_rows * tok_rows < channels
        and slab >= (KEYS - QUERY_WINDOW) // 2
    )
    if not fits:
        return spread_device(*args)
    side = (KEYS - QUERY_WINDOW) // 2
    args = list(args)
    for k in (1, 7, 8):
        args[k] = args[k].reshape(1, -1)
    args[11] = args[11].T
    agg_width = args[15].shape[1]
    sizes = (devices, tok_rows, tokens, channels, owned, slab, heads)
    in_vmem = pl.BlockSpec(memory_space=pltpu.VMEM)
    in_hbm = pl.BlockSpec(memory_space=pltpu.HBM)
    return tuple(
        pl.pallas_call(
            functools.partial(fused_kernel, sizes),
            out_shape=(
                pltpu.VMEM(pair.shape, BF16),
                pltpu.VMEM(atom_act.shape, BF16),
                pltpu.VMEM((tok_rows, agg_width), BF16),
            ),
            in_specs=[in_hbm] * len(args),
            out_specs=(in_vmem,) * 3,
            scratch_shapes=[
                pltpu.VMEM((2, devices * block, tokens), F32),
                pltpu.VMEM((devices, 2, block, tokens), BF16),
                pltpu.VMEM((devices, 2, block, tokens), BF16),
                pltpu.VMEM((devices * block, tokens), F32),
                pltpu.VMEM((devices * block, tokens), F32),
                pltpu.VMEM((devices * block, tokens), F32),
                pltpu.VMEM((devices, block, tokens), BF16),
                pltpu.VMEM((devices, block, tokens), BF16),
                pltpu.VMEM((tok_rows, tokens, channels), F32),
                pltpu.VMEM((slab + 2 * side, 3 * width), BF16),
                pltpu.SemaphoreType.DMA((2,)),
                pltpu.SemaphoreType.DMA((2,)),
                pltpu.SemaphoreType.DMA((2,)),
                pltpu.SemaphoreType.DMA((2,)),
                pltpu.SemaphoreType.DMA((len(args),)),
                *[pltpu.VMEM(a.shape, a.dtype) for a in args],
            ],
            compiler_params=pltpu.CompilerParams(
                collective_id=0, has_side_effects=True, vmem_limit_bytes=60 * 1024 * 1024
            ),
            name="triangle_atoms",
        )(*args)
    )


def solution(mesh):
    in_specs = (
        P(("groups", "row"), "col", None),
        P("groups"),
        P(),
        P(),
        P(),
        P(("groups", "row"), None),
        P(("groups", "row"), None),
        P(("groups", "row")),
        P(("groups", "row")),
        P(),
        P(),
        P(),
        P(),
        P(),
        P(),
        P(),
    )
    out_specs = (
        P(("groups", "row"), "col", None),
        P(("groups", "row"), None),
        P(("groups", "row"), None),
    )
    return jax.shard_map(
        per_device, mesh=mesh, in_specs=in_specs, out_specs=out_specs, check_vma=False
    )
```

```python
import functools
import math

import jax
import jax.numpy as jnp
from jax import lax
from jax.experimental import pallas as pl
from jax.experimental.pallas import tpu as pltpu
from jax.sharding import PartitionSpec as P

QUERY_WINDOW = 32
KEYS = 128


EPSILON = 1e-05


def extended(shard, sides, width):
    for axis, dim in sides:
        size, length = (lax.axis_size(axis), shard.shape[dim])
        up = [(i, (i + 1) % size) for i in range(size - 1)]
        down = [(j, i) for i, j in up]
        last = lax.slice_in_dim(shard, length - width, length, axis=dim)
        first = lax.slice_in_dim(shard, 0, width, axis=dim)
        before = lax.ppermute(last, axis, up)
        after = lax.ppermute(first, axis, down)
        shard = jnp.concatenate([before, shard, after], axis=dim)
    return shard


def layer_norm(values, along):
    average = jnp.mean(values, axis=along, keepdims=True)
    centred = values - average
    spread = jnp.mean(centred * centred, axis=along, keepdims=True)
    return centred / jnp.sqrt(spread + EPSILON)


def spread_device(
    pair,
    token_mask,
    tri_in_weight,
    tri_gate_weight,
    tri_out_weight,
    atom_act,
    atom_cond,
    atom_token,
    atom_mask,
    ada_weight,
    qkv_weight,
    bias_weight,
    attn_out_weight,
    ffn_in_weight,
    ffn_out_weight,
    agg_weight,
):
    tok_rows = pair.shape[0]
    col_count = pair.shape[1]
    channels = pair.shape[2]
    row_index = lax.axis_index("row")
    col_index = lax.axis_index("col")
    pair_float = pair.astype(jnp.float32)
    pair_norm = layer_norm(pair_float, 2).astype(jnp.bfloat16)
    row_live = lax.dynamic_slice_in_dim(token_mask, row_index * tok_rows, tok_rows, 0).astype(
        jnp.float32
    )
    col_live = lax.dynamic_slice_in_dim(token_mask, col_index * col_count, col_count, 0).astype(
        jnp.float32
    )
    pair_live = row_live[:, None] * col_live[None, :]
    left_terms = jnp.einsum(
        "ijd,de->eij",
        pair_norm,
        tri_in_weight[:, : 2 * channels],
        preferred_element_type=jnp.float32,
    )
    left = (jax.nn.sigmoid(left_terms[channels:]) * left_terms[:channels] * pair_live).astype(
        jnp.bfloat16
    )
    right_terms = jnp.einsum(
        "ijd,de->eij",
        pair_norm,
        tri_in_weight[:, 2 * channels :],
        preferred_element_type=jnp.float32,
    )
    right = (jax.nn.sigmoid(right_terms[channels:]) * right_terms[:channels] * pair_live).astype(
        jnp.bfloat16
    )
    tri_gate = jax.nn.sigmoid(
        jnp.einsum("ijd,de->ije", pair_norm, tri_gate_weight, preferred_element_type=jnp.float32)
    )
    left_owned, right_owned = (
        lax.all_to_all(left, "row", split_axis=0, concat_axis=1, tiled=True),
        lax.all_to_all(right, "row", split_axis=0, concat_axis=1, tiled=True),
    )
    left_full, right_rows = (
        lax.all_gather(left_owned, "col", axis=2, tiled=True),
        lax.all_gather(right_owned, "col", axis=2, tiled=True),
    )
    right_used = lax.dynamic_slice_in_dim(right_rows, col_index * col_count, col_count, 1)
    tri_sum = jnp.einsum(
        "cik,cjk->cij", left_full, right_used, preferred_element_type=jnp.float32
    ).astype(jnp.bfloat16)
    merged = lax.all_to_all(tri_sum, "row", split_axis=1, concat_axis=0, tiled=True)
    tri_norm = layer_norm(merged.astype(jnp.float32), 0).astype(jnp.bfloat16)
    update = jnp.einsum("dij,de->ije", tri_norm, tri_out_weight, preferred_element_type=jnp.float32)
    pair_out = (pair_float + tri_gate * update).astype(jnp.bfloat16)
    band_width = 3 * tok_rows
    targets = (row_index - 1) * tok_rows + jnp.arange(band_width, dtype=jnp.int32)
    columns = col_index * col_count + jnp.arange(col_count, dtype=jnp.int32)
    selector = (columns[:, None] == targets[None, :]).astype(jnp.bfloat16)
    band_part = jnp.einsum("ijd,jb->ibd", pair_out, selector, preferred_element_type=jnp.float32)
    band = lax.psum(band_part.astype(jnp.bfloat16), "col").astype(jnp.float32)
    band_norm = layer_norm(band, 2).astype(jnp.bfloat16)
    bias_table = jnp.einsum(
        "ibd,dh->ibh", band_norm, bias_weight, preferred_element_type=jnp.float32
    ).astype(jnp.bfloat16)
    slab = atom_act.shape[0]
    window_width = atom_act.shape[1]
    heads = bias_weight.shape[1]
    head_size = window_width // heads
    side = (KEYS - QUERY_WINDOW) // 2
    windows = slab // QUERY_WINDOW
    local_token = atom_token - row_index * tok_rows
    live = atom_mask.astype(jnp.float32)
    token_tag = ((local_token + 1) * atom_mask).astype(jnp.bfloat16)
    ada = jnp.dot(atom_cond, ada_weight, preferred_element_type=jnp.float32)
    atom_inputs = (
        jax.nn.sigmoid(ada[:, :window_width]) * layer_norm(atom_act.astype(jnp.float32), 1)
        + ada[:, window_width:]
    ).astype(jnp.bfloat16)
    projected = jnp.dot(atom_inputs, qkv_weight, preferred_element_type=jnp.float32).astype(
        jnp.bfloat16
    )
    queries = projected[:, :window_width]
    ext_pairs, ext_tag = (
        extended(projected[:, window_width:], (("row", 0),), side),
        extended(token_tag, (("row", 0),), side),
    )
    ext_rows = slab + 2 * side
    ext_position = jnp.arange(ext_rows, dtype=jnp.int32)
    offset = jnp.where(
        ext_position < side, 0, jnp.where(ext_position < side + slab, tok_rows, 2 * tok_rows)
    )
    tag_value = ext_tag.astype(jnp.int32)
    key_valid = tag_value > 0
    band_index = tag_value - 1 + offset
    band_slots = jnp.arange(band_width, dtype=jnp.int32)
    key_onehot = ((band_index[:, None] == band_slots[None, :]) & key_valid[:, None]).astype(
        jnp.bfloat16
    )
    query_onehot = (local_token[:, None] == jnp.arange(tok_rows, dtype=jnp.int32)[None, :]).astype(
        jnp.bfloat16
    )
    query_bias = jnp.einsum(
        "lt,tbh->lbh", query_onehot, bias_table, preferred_element_type=jnp.float32
    ).astype(jnp.bfloat16)
    query_bias = query_bias.reshape(windows, QUERY_WINDOW, band_width, heads)
    key_index = (
        jnp.arange(windows, dtype=jnp.int32)[:, None] * QUERY_WINDOW
        + jnp.arange(KEYS, dtype=jnp.int32)[None, :]
    )
    window_pairs = ext_pairs[key_index]
    window_onehot = key_onehot[key_index]
    window_valid = key_valid[key_index]
    window_bias = jnp.einsum(
        "wlbh,wmb->whlm", query_bias, window_onehot, preferred_element_type=jnp.float32
    )
    query_heads = queries.reshape(windows, QUERY_WINDOW, heads, head_size)
    key_heads = window_pairs[..., :window_width].reshape(windows, KEYS, heads, head_size)
    value_heads = window_pairs[..., window_width:].reshape(windows, KEYS, heads, head_size)
    logit_scores = (
        jnp.einsum("wlhd,wmhd->whlm", query_heads, key_heads, preferred_element_type=jnp.float32)
        / math.sqrt(head_size)
        + window_bias
    )
    logit_scores = jnp.where(window_valid[:, None, None, :], logit_scores, -1e30)
    attn_weights = jax.nn.softmax(logit_scores, axis=-1).astype(jnp.bfloat16)
    attended = (
        jnp.einsum("whlm,wmhd->wlhd", attn_weights, value_heads, preferred_element_type=jnp.float32)
        .reshape(slab, window_width)
        .astype(jnp.bfloat16)
    )
    atom_mid = atom_act.astype(jnp.float32) + jnp.dot(
        attended, attn_out_weight, preferred_element_type=jnp.float32
    )
    atom_norm = layer_norm(atom_mid, 1).astype(jnp.bfloat16)
    expanded = jnp.dot(atom_norm, ffn_in_weight, preferred_element_type=jnp.float32)
    hidden_width = ffn_out_weight.shape[0]
    inner = (jax.nn.silu(expanded[:, :hidden_width]) * expanded[:, hidden_width:]).astype(
        jnp.bfloat16
    )
    atom_out = (
        (atom_mid + jnp.dot(inner, ffn_out_weight, preferred_element_type=jnp.float32))
        * live[:, None]
    ).astype(jnp.bfloat16)
    features = jax.nn.relu(
        jnp.dot(atom_out, agg_weight, preferred_element_type=jnp.float32)
    ).astype(jnp.bfloat16)
    live_onehot = query_onehot * atom_mask.astype(jnp.bfloat16)[:, None]
    token_sums = jnp.einsum("at,ac->tc", live_onehot, features, preferred_element_type=jnp.float32)
    token_counts = jnp.sum(live_onehot.astype(jnp.float32), axis=0)
    token_out = (token_sums / token_counts[:, None]).astype(jnp.bfloat16)
    return (pair_out, atom_out, token_out)


MESH = pl.DeviceIdType.MESH
F32 = jnp.float32
BF16 = jnp.bfloat16


def dot_nn(a, b):
    return lax.dot_general(a, b, (((1,), (0,)), ((), ())), preferred_element_type=F32)


def dot_nt(a, b):
    return lax.dot_general(a, b, (((1,), (1,)), ((), ())), preferred_element_type=F32)


def dot_tn(a, b):
    return lax.dot_general(a, b, (((0,), (0,)), ((), ())), preferred_element_type=F32)


def normed(values, along):
    average = jnp.mean(values, axis=along, keepdims=True)
    centred = values - average
    spread = jnp.mean(centred * centred, axis=along, keepdims=True)
    return centred * lax.rsqrt(spread + EPSILON)


FETCH_ORDER = (0, 2, 1, 3, 6, 9, 5, 7, 8, 10, 4, 11, 12, 13, 14, 15)


def fused_kernel(
    sizes,
    *refs,
):
    count = len(FETCH_ORDER)
    operands, refs = refs[:count], refs[count:]
    (
        pair_out,
        atom_out,
        token_out,
        terms_wide,
        send_terms,
        recv_terms,
        left_wide,
        right_wide,
        sums_wide,
        send_sums,
        recv_sums,
        gate_ref,
        rim,
        send_sem,
        recv_sem,
        rim_send,
        rim_recv,
        fetch_sem,
    ) = refs[: len(refs) - count]
    held = refs[len(refs) - count :]
    fetches = [
        pltpu.make_async_copy(operands[k], held[k], fetch_sem.at[k]) for k in range(count)
    ]
    for k in FETCH_ORDER:
        fetches[k].start()
    (
        pair,
        token_mask,
        tri_in_weight,
        tri_gate_weight,
        tri_out_weight,
        atom_act,
        atom_cond,
        atom_token,
        atom_mask,
        ada_weight,
        qkv_weight,
        bias_weight,
        attn_out_weight,
        ffn_in_weight,
        ffn_out_weight,
        agg_weight,
    ) = held
    devices, tok_rows, tokens, channels, owned, slab, heads = sizes
    block = tok_rows * owned
    side = (KEYS - QUERY_WINDOW) // 2
    ext = slab + 2 * side
    group = lax.axis_index("groups")
    me = lax.axis_index("row")
    col = lax.axis_index("col")

    barrier = pltpu.get_barrier_semaphore()

    def greet(step, carry):
        peer = lax.rem(me + step, devices)
        pl.semaphore_signal(barrier, inc=1, device_id=(group, peer, col), device_id_type=MESH)
        return carry

    lax.fori_loop(1, devices, greet, 0)

    for k in (0, 2, 1, 3):
        fetches[k].wait()
    mask_row = token_mask[...].astype(F32)
    lane = lax.broadcasted_iota(jnp.int32, (1, tokens), 1)
    in_weight = tri_in_weight[...].T
    for i in range(tok_rows):
        norm = normed(pair[i].astype(F32), 1).astype(BF16)
        row_mask = jnp.sum(jnp.where(lane == me * tok_rows + i, mask_row, 0.0), axis=1, keepdims=True)
        both = row_mask * mask_row
        terms = dot_nt(in_weight, norm)
        for part in range(2):
            base = part * 2 * channels
            value = (
                jax.nn.sigmoid(terms[base + channels : base + 2 * channels])
                * terms[base : base + channels]
                * both
            )
            for c in range(owned):
                terms_wide[part, pl.ds(i * owned + c, devices, stride=block), :] = value[
                    c * devices : (c + 1) * devices
                ]
        gate_ref[i] = jax.nn.sigmoid(dot_nn(norm, tri_gate_weight[...]))
    for part in range(2):
        send_terms[:, part] = terms_wide[part].reshape(devices, block, tokens).astype(BF16)

    pl.semaphore_wait(barrier, devices - 1)

    def terms_copy(peer):
        return pltpu.make_async_remote_copy(
            src_ref=send_terms.at[peer],
            dst_ref=recv_terms.at[me],
            send_sem=send_sem.at[0],
            recv_sem=recv_sem.at[0],
            device_id=(group, peer, col),
            device_id_type=MESH,
        )

    def send_first(pair_step, carry):
        terms_copy(lax.rem(me + pair_step, devices)).start()
        terms_copy(lax.rem(me + devices - pair_step, devices)).start()
        return carry

    lax.fori_loop(1, devices // 2, send_first, 0)
    terms_copy(lax.rem(me + devices // 2, devices)).start()
    recv_terms[me] = send_terms[me]

    for k in (6, 9, 5, 7, 8, 10):
        fetches[k].wait()
    token_row = atom_token[...] - me * tok_rows
    live_row = atom_mask[...]
    wide = (channels, slab)
    token_col = jnp.broadcast_to(token_row.astype(F32), wide).T
    live_col = jnp.broadcast_to(live_row.astype(F32), wide).T
    act = atom_act[...].astype(F32)
    ada = dot_nn(atom_cond[...], ada_weight[...])
    width = act.shape[1]
    atom_inputs = (jax.nn.sigmoid(ada[:, :width]) * normed(act, 1) + ada[:, width:]).astype(BF16)
    projected = dot_nn(atom_inputs, qkv_weight[...]).astype(BF16)
    rim[side : side + slab, : 2 * width] = projected[:, width:]
    rim[side : side + slab, 2 * width :] = ((token_col + 1.0) * live_col).astype(BF16)

    up = pltpu.make_async_remote_copy(
        src_ref=rim.at[pl.ds(slab, side)],
        dst_ref=rim.at[pl.ds(0, side)],
        send_sem=rim_send.at[0],
        recv_sem=rim_recv.at[0],
        device_id=(group, lax.rem(me + 1, devices), col),
        device_id_type=MESH,
    )
    down = pltpu.make_async_remote_copy(
        src_ref=rim.at[pl.ds(side, side)],
        dst_ref=rim.at[pl.ds(side + slab, side)],
        send_sem=rim_send.at[1],
        recv_sem=rim_recv.at[1],
        device_id=(group, lax.rem(me + devices - 1, devices), col),
        device_id_type=MESH,
    )

    @pl.when(me < devices - 1)
    def _():
        up.start()

    @pl.when(me > 0)
    def _():
        down.start()

    @pl.when(me == 0)
    def _():
        rim[:side] = jnp.zeros((side, rim.shape[1]), BF16)

    @pl.when(me == devices - 1)
    def _():
        rim[side + slab :] = jnp.zeros((side, rim.shape[1]), BF16)

    others = pl.ds(0, devices - 1)
    pltpu.make_async_copy(send_terms.at[others], recv_terms.at[others], recv_sem.at[0]).wait()
    left_wide[...] = recv_terms[:, 0].reshape(devices * block, tokens).astype(F32)
    right_wide[...] = recv_terms[:, 1].reshape(devices * block, tokens).astype(F32)
    for c in range(owned):
        rows = pl.ds(c, tokens, stride=owned)
        sums_wide[rows, :] = dot_nt(
            left_wide[rows, :].astype(BF16), right_wide[rows, :].astype(BF16)
        )
    send_sums[...] = sums_wide[...].reshape(devices, block, tokens).astype(BF16)

    def sums_copy(peer):
        return pltpu.make_async_remote_copy(
            src_ref=send_sums.at[peer],
            dst_ref=recv_sums.at[me],
            send_sem=send_sem.at[1],
            recv_sem=recv_sem.at[1],
            device_id=(group, peer, col),
            device_id_type=MESH,
        )

    def send_second(pair_step, carry):
        sums_copy(lax.rem(me + pair_step, devices)).start()
        sums_copy(lax.rem(me + devices - pair_step, devices)).start()
        return carry

    lax.fori_loop(1, devices // 2, send_second, 0)
    sums_copy(lax.rem(me + devices // 2, devices)).start()
    recv_sums[me] = send_sums[me]

    @pl.when(me > 0)
    def _():
        up.wait_recv()

    @pl.when(me < devices - 1)
    def _():
        down.wait_recv()

    head_size = width // heads
    keys = rim[:, :width]
    values = rim[:, width : 2 * width]
    tag = rim[:, 2 * width :].astype(F32)
    head_lane = lax.broadcasted_iota(jnp.int32, (slab, width), 1) // head_size
    queries = projected[:, :width].astype(F32)
    split_queries = jnp.concatenate(
        [jnp.where(head_lane == h, queries, 0.0) for h in range(heads)], axis=0
    ).astype(BF16)
    raw_scores = dot_nt(split_queries, keys) * (1.0 / math.sqrt(head_size))
    band = 4 * tok_rows
    dead_lane = tok_rows * band
    ext_row = lax.broadcasted_iota(jnp.int32, (ext, channels), 0)
    ext_lane = lax.broadcasted_iota(jnp.int32, (ext, channels), 1)
    offset = jnp.where(
        ext_row < side, 0, jnp.where(ext_row < side + slab, tok_rows, 2 * tok_rows)
    )
    band_index = tag.astype(jnp.int32) - 1 + offset
    slot = lax.rem(ext_lane, band)
    alive = tag > 0.0
    key_map = jnp.where(
        ext_lane < dead_lane,
        jnp.where(alive & (band_index == slot), 1.0, 0.0),
        jnp.where(alive, 0.0, 1.0),
    ).astype(BF16)
    query_lane = lax.broadcasted_iota(jnp.int32, (slab, channels), 1)
    query_map = jnp.where(
        (query_lane // band == token_col.astype(jnp.int32)) | (query_lane == dead_lane), 1.0, 0.0
    )
    score_row = lax.broadcasted_iota(jnp.int32, (slab, ext), 0) // QUERY_WINDOW * QUERY_WINDOW
    score_lane = lax.broadcasted_iota(jnp.int32, (slab, ext), 1)
    in_window = (score_lane >= score_row) & (score_lane < score_row + KEYS)

    for k in (4, 11, 12, 13, 14, 15):
        fetches[k].wait()
    pltpu.make_async_copy(send_sums.at[others], recv_sums.at[others], recv_sem.at[1]).wait()
    sums_wide[...] = recv_sums[...].reshape(devices * block, tokens).astype(F32)
    band_row = lax.broadcasted_iota(jnp.int32, (band, tokens), 0)
    band_lane = lax.broadcasted_iota(jnp.int32, (band, tokens), 1)
    selector = jnp.where(
        (band_lane == (me - 1) * tok_rows + band_row) & (band_row < 3 * tok_rows), 1.0, 0.0
    ).astype(BF16)
    bands = []
    for i in range(tok_rows):
        merged = jnp.concatenate(
            [
                sums_wide[pl.ds(i * owned + c, devices, stride=block), :]
                for c in range(owned)
            ],
            axis=0,
        )
        tri_norm = normed(merged, 0).T.astype(BF16)
        update = dot_nn(tri_norm, tri_out_weight[...])
        updated = (pair[i].astype(F32) + gate_ref[i] * update).astype(BF16)
        pair_out[i] = updated
        bands.append(dot_nn(selector, updated))
    bands.append(jnp.zeros((channels - tok_rows * band, channels), F32))
    band_norm = normed(jnp.concatenate(bands, axis=0), 1).astype(BF16)
    table = dot_nt(bias_weight[...], band_norm).astype(BF16).astype(F32)
    table_lane = lax.broadcasted_iota(jnp.int32, table.shape, 1)
    table = jnp.where(table_lane == dead_lane, -1e30, table)
    bias_rows = jnp.concatenate(
        [query_map * table[h : h + 1] for h in range(heads)], axis=0
    ).astype(BF16)
    scores = raw_scores + dot_nt(bias_rows, key_map)
    scores = jnp.where(jnp.concatenate([in_window] * heads, axis=0), scores, -1e30)
    scores = jnp.exp(scores - jnp.max(scores, axis=1, keepdims=True))
    weights = (scores / jnp.sum(scores, axis=1, keepdims=True)).astype(BF16)
    mixed = dot_nn(weights, values)
    attended = jnp.zeros((slab, width), F32)
    for h in range(heads):
        attended = jnp.where(head_lane == h, mixed[h * slab : (h + 1) * slab], attended)
    atom_mid = act + dot_nn(attended.astype(BF16), attn_out_weight[...])
    expanded = dot_nn(normed(atom_mid, 1).astype(BF16), ffn_in_weight[...])
    hidden = ffn_out_weight.shape[0]
    up_part, gate_part = expanded[:, hidden:], expanded[:, :hidden]
    inner = (gate_part * jax.nn.sigmoid(gate_part) * up_part).astype(BF16)
    result = ((atom_mid + dot_nn(inner, ffn_out_weight[...])) * live_col).astype(BF16)
    atom_out[...] = result
    features = jnp.maximum(dot_nn(result, agg_weight[...]), 0.0).astype(BF16)
    owner_row = lax.broadcasted_iota(jnp.int32, (tok_rows, slab), 0)
    owner = jnp.where((owner_row == token_row) & (live_row > 0), 1.0, 0.0)
    counts = jnp.sum(owner, axis=1, keepdims=True)
    token_out[...] = (dot_nn(owner.astype(BF16), features) / counts).astype(BF16)

    pltpu.make_async_copy(send_terms.at[others], recv_terms.at[others], send_sem.at[0]).wait()
    pltpu.make_async_copy(send_sums.at[others], recv_sums.at[others], send_sem.at[1]).wait()

    @pl.when(me < devices - 1)
    def _():
        up.wait_send()

    @pl.when(me > 0)
    def _():
        down.wait_send()


def per_device(*args):
    pair, token_mask, atom_act, atom_token = args[0], args[1], args[5], args[7]
    tok_rows, tokens, channels = pair.shape
    slab, width = atom_act.shape
    heads = args[11].shape[1]
    devices = lax.axis_size("row")
    owned = channels // devices
    block = tok_rows * owned
    fits = (
        lax.axis_size("col") == 1
        and owned * devices == channels
        and block % 16 == 0
        and slab % QUERY_WINDOW == 0
        and devices % 8 == 0
        and width == channels
        and 4 * tok_rows % 16 == 0
        and 4 * tok_rows * tok_rows < channels
        and slab >= (KEYS - QUERY_WINDOW) // 2
    )
    if not fits:
        return spread_device(*args)
    side = (KEYS - QUERY_WINDOW) // 2
    args = list(args)
    for k in (1, 7, 8):
        args[k] = args[k].reshape(1, -1)
    args[11] = args[11].T
    agg_width = args[15].shape[1]
    sizes = (devices, tok_rows, tokens, channels, owned, slab, heads)
    in_vmem = pl.BlockSpec(memory_space=pltpu.VMEM)
    in_hbm = pl.BlockSpec(memory_space=pltpu.HBM)
    return tuple(
        pl.pallas_call(
            functools.partial(fused_kernel, sizes),
            out_shape=(
                pltpu.VMEM(pair.shape, BF16),
                pltpu.VMEM(atom_act.shape, BF16),
                pltpu.VMEM((tok_rows, agg_width), BF16),
            ),
            in_specs=[in_hbm] * len(args),
            out_specs=(in_vmem,) * 3,
            scratch_shapes=[
                pltpu.VMEM((2, devices * block, tokens), F32),
                pltpu.VMEM((devices, 2, block, tokens), BF16),
                pltpu.VMEM((devices, 2, block, tokens), BF16),
                pltpu.VMEM((devices * block, tokens), F32),
                pltpu.VMEM((devices * block, tokens), F32),
                pltpu.VMEM((devices * block, tokens), F32),
                pltpu.VMEM((devices, block, tokens), BF16),
                pltpu.VMEM((devices, block, tokens), BF16),
                pltpu.VMEM((tok_rows, tokens, channels), F32),
                pltpu.VMEM((slab + 2 * side, 3 * width), BF16),
                pltpu.SemaphoreType.DMA((2,)),
                pltpu.SemaphoreType.DMA((2,)),
                pltpu.SemaphoreType.DMA((2,)),
                pltpu.SemaphoreType.DMA((2,)),
                pltpu.SemaphoreType.DMA((len(args),)),
                *[pltpu.VMEM(a.shape, a.dtype) for a in args],
            ],
            compiler_params=pltpu.CompilerParams(
                collective_id=0, has_side_effects=True, vmem_limit_bytes=60 * 1024 * 1024
            ),
            name="triangle_atoms",
        )(*args)
    )


def solution(mesh):
    in_specs = (
        P(("groups", "row"), "col", None),
        P("groups"),
        P(),
        P(),
        P(),
        P(("groups", "row"), None),
        P(("groups", "row"), None),
        P(("groups", "row")),
        P(("groups", "row")),
        P(),
        P(),
        P(),
        P(),
        P(),
        P(),
        P(),
    )
    out_specs = (
        P(("groups", "row"), "col", None),
        P(("groups", "row"), None),
        P(("groups", "row"), None),
    )
    return jax.shard_map(
        per_device, mesh=mesh, in_specs=in_specs, out_specs=out_specs, check_vma=False
    )
```
